128 devices in a mesh: dom: 32 (over x, y, z_hi), smp: 4 (over z_lo, core).
Axes of the slice: x: 4, y: 4, z: 4 (z_hi: 2, z_lo: 2; z = z_hi * 2 + z_lo), core: 2. Of those that a mesh axis runs over, the one named last changes fastest.
Arguments:
- state_before: float32 [4, 256, 128, 256], P('smp', 'dom'), may hold values from -6 to 6
- state_now: float32 [4, 256, 128, 256], P('smp', 'dom'), may hold values from -6 to 6
- base_model: float32 [256, 128, 256], P('dom'), may hold values from 0.06 to 0.16
- buoyancy: float32 [256, 128, 256], P('dom'), may hold values from 0.5 to 1.5
- latent: float32 [4, 256, 128, 256], P('smp', 'dom'), may hold values from -6 to 6
- flow_gain: bfloat16 [256, 128, 256], P('dom', 'smp'), may hold values from -6 to 6
- flow_bias: bfloat16 [256, 128, 256], P('dom', 'smp'), may hold values from -3 to 3
- records: bfloat16 [64, 4, 256, 128], P('dom'), may hold values from -6 to 6
- source_wavelet: float32 [64, 4], replicated, may hold values from -32 to 32
- source_cell: int32 [64], replicated, may hold values from 0 to 8388607
- shot: int32 [1], replicated, may hold values from 0 to 63
- receiver_depth: int32 [256, 128], P('dom'), may hold values from 1 to 254
Outputs:
- image: float32 [4, 256, 128, 256], P('smp', 'dom')
- gain_grad: float32 [256, 128, 256], P('dom', 'smp')
- bias_grad: float32 [256, 128, 256], P('dom', 'smp')
The draws below stay inside these ranges and needn't reach their ends.
All inputs are finite; a program needn't handle non-finite values.
Results may differ from the reference program's by a relative error of at most 0.0003.
Values may be sent and summed in bfloat16 or wider, within the bound.
A program may use at most 64 MiB of HBM per device.

```python
import jax
import jax.numpy as jnp
from jax import lax

NY = 128
NZ = 256
STEPS = 4
NX = 256
SHOTS = 64
SAMPLES = 4


def set_ends(entries, own_key, smallest, largest):
    longest = entries.shape.index(max(entries.shape))
    spots = []
    for shift in (0, 1):
        where = [jax.random.randint(jax.random.fold_in(own_key, axis), (), 0, length) for axis, length in enumerate(entries.shape)]
        where[longest] = (where[longest] + shift) % entries.shape[longest]
        spots.append(tuple(where))
    return entries.at[spots[0]].set(smallest).at[spots[1]].set(largest)


def block_levels(own_key, shape, split, low, largest):
    level = 1.0
    for position, shards_of in split:
        steps = jax.random.uniform(jax.random.fold_in(jax.random.fold_in(own_key, 6), position), (shards_of,), jnp.float32, low / len(split), largest / len(split))
        level = level * jnp.repeat(jnp.exp(steps), shape[position] // shards_of).reshape((-1,) + (1,) * (len(shape) - 1 - position))
    return level


def normal_values(stream_key, extent, width, bound, pieces=(), kind=jnp.bfloat16):
    drawn = width * jax.random.normal(stream_key, extent, jnp.float32)
    if pieces:
        drawn = drawn * block_levels(stream_key, extent, pieces, -0.22, 0.18)
    return jnp.clip(drawn, -bound, bound).astype(kind)


def setup_inputs(seed: int = 0) -> dict:
    key_of = jax.random.split(jax.random.key(seed), 13)
    return {
        "state_before": normal_values(key_of[0], (SAMPLES, NX, NY, NZ), 1.0, 6.0, ((0, 4), (1, 32)), jnp.float32),
        "state_now": normal_values(key_of[1], (SAMPLES, NX, NY, NZ), 1.0, 6.0, ((0, 4), (1, 32)), jnp.float32),
        "base_model": jnp.clip(0.06 + 0.09999999776482582 * jax.random.uniform(key_of[2], (NX, NY, NZ), jnp.float32) ** block_levels(key_of[2], (NX, NY, NZ), ((0, 32),), -0.2, 0.2), 0.06, 0.16),
        "buoyancy": jnp.clip(0.5 + 1.0 * jax.random.uniform(key_of[3], (NX, NY, NZ), jnp.float32) ** block_levels(key_of[3], (NX, NY, NZ), ((0, 32),), -0.2, 0.2), 0.5, 1.5),
        "latent": normal_values(key_of[4], (SAMPLES, NX, NY, NZ), 1.0, 6.0, ((0, 4), (1, 32)), jnp.float32),
        "flow_gain": normal_values(key_of[5], (NX, NY, NZ), 1.0, 6.0, ((0, 32), (1, 4))),
        "flow_bias": normal_values(key_of[6], (NX, NY, NZ), 0.5, 3.0, ((0, 32), (1, 4))),
        "records": normal_values(key_of[7], (SHOTS, STEPS, NX, NY), 1.0, 6.0, ((0, 32),)),
        "source_wavelet": normal_values(key_of[8], (SHOTS, STEPS), 5.0, 32.0, (), jnp.float32),
        "source_cell": set_ends(jax.random.randint(key_of[9], (SHOTS,), 0, NX * NY * NZ), jax.random.fold_in(key_of[9], 1), 0, (NX * NY * NZ) - 1).astype(jnp.int32),
        "shot": jax.random.randint(key_of[10], (1,), 0, SHOTS).astype(jnp.int32),
        "receiver_depth": set_ends(jax.random.randint(key_of[11], (NX, NY), 1, NZ - 1), jax.random.fold_in(key_of[11], 1), 1, (NZ - 1) - 1).astype(jnp.int32),
    }


def operate_padded(field, buoy):
    middle = field[1:-1]
    middle_buoy = buoy[1:-1]
    total = 0.5 * (middle_buoy + buoy[2:]) * (field[2:] - middle) + 0.5 * (middle_buoy + buoy[:-2]) * (field[:-2] - middle)
    side_field = jnp.pad(middle, ((0, 0), (1, 1), (0, 0)))
    side_buoy = jnp.pad(middle_buoy, ((0, 0), (1, 1), (0, 0)))
    total = total + 0.5 * (middle_buoy + side_buoy[:, 2:]) * (side_field[:, 2:] - middle) + 0.5 * (middle_buoy + side_buoy[:, :-2]) * (side_field[:, :-2] - middle)
    deep_field = jnp.pad(middle, ((0, 0), (0, 0), (1, 1)))
    deep_buoy = jnp.pad(middle_buoy, ((0, 0), (0, 0), (1, 1)))
    total = total + 0.5 * (middle_buoy + deep_buoy[:, :, 2:]) * (deep_field[:, :, 2:] - middle) + 0.5 * (middle_buoy + deep_buoy[:, :, :-2]) * (deep_field[:, :, :-2] - middle)
    return total


def operate(field, buoy):
    widths = ((1, 1), (0, 0), (0, 0))
    return operate_padded(jnp.pad(field, widths), jnp.pad(buoy, widths))


def reference(state_before, state_now, base_model, buoyancy, latent, flow_gain, flow_bias, records, source_wavelet, source_cell, shot, receiver_depth):
    picked = shot[0]
    record = lax.dynamic_index_in_dim(records, picked, 0, keepdims=False).astype(jnp.float32)
    wavelet = lax.dynamic_index_in_dim(source_wavelet, picked, 0, keepdims=False)
    flat_cell = lax.dynamic_index_in_dim(source_cell, picked, 0, keepdims=False)
    cell_x = flat_cell // (NY * NZ)
    cell_y = (flat_cell // NZ) % NY
    cell_z = flat_cell % NZ
    point = ((jnp.arange(NX)[:, None, None] == cell_x) & (jnp.arange(NY)[None, :, None] == cell_y) & (jnp.arange(NZ)[None, None, :] == cell_z)).astype(jnp.float32)
    onehot = (jnp.arange(NZ)[None, None, :] == receiver_depth[:, :, None]).astype(jnp.float32)
    gain = flow_gain.astype(jnp.float32)
    bias = flow_bias.astype(jnp.float32)
    gain_total = jnp.zeros(base_model.shape, jnp.float32)
    bias_total = jnp.zeros(base_model.shape, jnp.float32)
    images = []
    for member in range(SAMPLES):
        squash = jnp.tanh(latent[member] * gain + bias)
        model = base_model * jnp.exp(0.25 * squash)
        previous = state_before[member]
        current = state_now[member]
        images_of_state = []
        residuals = []
        for turn in range(STEPS):
            applied = operate(current, buoyancy)
            images_of_state.append(applied)
            following = 2.0 * current - previous + model * applied + wavelet[turn] * point
            residuals.append(jnp.sum(following * onehot, axis=2) - record[turn])
            previous = current
            current = following
        later = jnp.zeros(base_model.shape, jnp.float32)
        latest = jnp.zeros(base_model.shape, jnp.float32)
        image = jnp.zeros(base_model.shape, jnp.float32)
        for turn in reversed(range(STEPS)):
            adjoint = 2.0 * later - latest + operate(model * later, buoyancy) + residuals[turn][:, :, None] * onehot
            image = image + adjoint * images_of_state[turn]
            latest = later
            later = adjoint
        common = image * model * 0.25 * (1.0 - squash * squash)
        gain_total = gain_total + common * latent[member]
        bias_total = bias_total + common
        images.append(image)
    return jnp.stack(images), gain_total, bias_total
```

```python
import functools

import jax
import jax.numpy as jnp
from jax import lax
from jax.experimental import pallas as pl
from jax.experimental.pallas import tpu as pltpu
from jax.sharding import PartitionSpec as P

MESH = pl.DeviceIdType.MESH
F32 = jnp.float32
PAD = 8
T = 8


def kernel(
    sb_h, sn_h, base_h, buoy_h, lat_h, gain_h, bias_h, rec_h, wav, cell, shot, depth,
    img_h, gg_h, bg_h,
    U, W, B, SB, BASE, LAT, PG, RQ, LU, U5, M, Q, CX, CY, CZP, CZM, DB, RB, HIT, AA, IMG, CG, RA, RBUF, RX, RY, RZ, RS, RALL,
    lsem, bar_dummy, hs, hr, ps, pr, gs, gr, rs, rr,
):
    d = lax.axis_index("dom")
    s = lax.axis_index("smp")
    gx, gy, gz = d // 8, (d // 2) % 4, d % 2
    zl, c = s // 2, s % 2
    left, right = ((d + 31) % 32, s), ((d + 1) % 32, s)
    core = (d, 2 * zl + (1 - c))
    zlo = (d, 2 * (1 - zl) + c)
    far = (d, 2 * (1 - zl) + (1 - c))
    xs = [(((gx + k) % 4) * 8 + d % 8, s) for k in (1, 2, 3)]
    ys = [(gx * 8 + ((gy + k) % 4) * 2 + gz, s) for k in (1, 2, 3)]
    zs = (d - gz + (1 - gz), s)

    def load(i, src, dst):
        cp = pltpu.make_async_copy(src, dst, lsem.at[i])
        cp.start()
        return cp

    rows = pl.ds(PAD, 128)
    inner = pl.ds(1, 8)
    ld_u = load(0, sn_h, U.at[0, inner, rows])
    ld_b = load(1, buoy_h, B.at[inner, rows])
    ld_g = load(2, gain_h, PG.at[s, 0])
    ld_c = load(3, bias_h, PG.at[s, 1])
    ld_r = load(4, rec_h.at[:, s], RQ)
    ld_base = load(5, base_h, BASE)
    ld_lat = load(6, lat_h, LAT)
    ld_sb = load(7, sb_h, SB)

    barrier = pltpu.get_barrier_semaphore()
    peers = [left, right, core, zlo, far] + xs + ys
    for p in peers:
        pl.semaphore_signal(barrier, inc=1, device_id=p, device_id_type=MESH)

    zero = jnp.zeros((T, 256), F32)

    def clear(i, _):
        for n in range(4):
            U[n, i, 0:8] = zero
            U[n, i, 136:144] = zero
        for n in range(3):
            W[n, i, 0:8] = zero
            W[n, i, 136:144] = zero
        B[i, 0:8] = zero
        B[i, 136:144] = zero
        return 0

    lax.fori_loop(0, 10, clear, 0)

    picked = shot[0]
    flat = cell[picked]
    cell_x = flat // (128 * 256)
    cell_y = (flat // 256) % 128
    cell_z = flat % 256
    lane = lax.broadcasted_iota(jnp.int32, (T, 256), 1)
    lane_f = lane.astype(F32)
    sub = lax.broadcasted_iota(jnp.int32, (T, 256), 0)
    for j in range(16):
        HIT[T * j : T * j + T] = jnp.where((sub + T * j == cell_y) & (lane == cell_z), 1.0, 0.0)
    dt = jnp.transpose(jnp.concatenate([depth[...].astype(F32), jnp.zeros((120, 128), F32)], axis=0))
    for x in range(8):
        DB[x] = jnp.broadcast_to(dt[:, x : x + 1], (128, 128))

    pl.semaphore_wait(barrier, len(peers))

    def rcopy(src, dst, ss, sr, dev):
        return pltpu.make_async_remote_copy(
            src_ref=src, dst_ref=dst, send_sem=ss, recv_sem=sr, device_id=dev, device_id_type=MESH
        )

    def halo(buf, i):
        a = rcopy(buf.at[8, rows], buf.at[0, rows], hs.at[i, 0], hr.at[i, 0], right)
        b = rcopy(buf.at[1, rows], buf.at[9, rows], hs.at[i, 1], hr.at[i, 1], left)
        a.start()
        b.start()
        return a, b

    def halo_wait(buf, cps):
        for cp in cps:
            cp.wait()

        @pl.when(d == 0)
        def _():
            for j in range(16):
                buf[0, PAD + T * j : PAD + T * j + T] = zero

        @pl.when(d == 31)
        def _():
            for j in range(16):
                buf[9, PAD + T * j : PAD + T * j + T] = zero

    ld_g.wait()
    ld_c.wait()
    p_z = rcopy(PG.at[s], PG.at[s], ps.at[0], pr.at[0], zlo)
    p_c = rcopy(PG.at[s], PG.at[s], ps.at[1], pr.at[1], core)
    p_z.start()
    p_c.start()
    ld_u.wait()
    h_u = halo(U.at[0], 0)
    ld_b.wait()
    h_b = halo(B, 1)

    ld_r.wait()
    mine = (picked // 2 == d).astype(F32)
    odd = (picked % 2).astype(F32)
    for k in range(4):
        r0 = RQ[0, 64 * k : 64 * k + 64].astype(F32)
        r1 = RQ[1, 64 * k : 64 * k + 64].astype(F32)
        RX[k] = (r0 * (1.0 - odd) + r1 * odd) * mine
    r_x = []
    for k in (1, 2, 3):
        cp = rcopy(RX.at[(gx + k) % 4], RX.at[3 + k], rs.at[k - 1], rr.at[k - 1], xs[k - 1])
        cp.start()
        r_x.append(cp)

    ld_base.wait()
    ld_lat.wait()
    ld_sb.wait()

    p_z.wait_recv()
    other = 2 * (1 - zl) + c
    p_f = rcopy(PG.at[other], PG.at[other], ps.at[2], pr.at[2], core)
    p_f.start()
    for cp in h_u:
        cp.wait()
    for cp in h_b:
        cp.wait()

    @pl.when(d == 0)
    def _():
        for j in range(16):
            U[0, 0, PAD + T * j : PAD + T * j + T] = zero
            B[0, PAD + T * j : PAD + T * j + T] = zero

    @pl.when(d == 31)
    def _():
        for j in range(16):
            U[0, 9, PAD + T * j : PAD + T * j + T] = zero
            B[9, PAD + T * j : PAD + T * j + T] = zero

    def coefs(x, _):
        for j in range(17):
            lo = PAD + T * j
            b = B[x + 1, lo : lo + T]
            CY[x, T * j : T * j + T] = 0.5 * (b + B[x + 1, lo - 1 : lo - 1 + T])
            if j < 16:
                CX[x, T * j : T * j + T] = 0.5 * (b + B[x, lo : lo + T])
                zn = jnp.where(lane == 255, 0.0, pltpu.roll(b, 255, 1))
                zp = jnp.where(lane == 0, 0.0, pltpu.roll(b, 1, 1))
                CZP[x, T * j : T * j + T] = 0.5 * (b + zn)
                CZM[x, T * j : T * j + T] = 0.5 * (b + zp)
        return 0

    lax.fori_loop(0, 8, coefs, 0)
    for j in range(16):
        lo = PAD + T * j
        CX[8, T * j : T * j + T] = 0.5 * (B[9, lo : lo + T] + B[8, lo : lo + T])

    r_a = r_x
    for cp in r_a:
        cp.wait()
    for k in range(4):
        sl = pl.ds(16 * k, 16)
        RY[k] = RX[gx, sl] + RX[4, sl] + RX[5, sl] + RX[6, sl]
    r_y = []
    for k in (1, 2, 3):
        cp = rcopy(RY.at[(gy + k) % 4], RY.at[3 + k], rs.at[2 + k], rr.at[2 + k], ys[k - 1])
        cp.start()
        r_y.append(cp)

    p_c.wait()
    p_f.wait()
    p_z.wait_send()

    def model(x, _):
        for j in range(8):
            k, o = j // 2, (j % 2) * 16
            sl = slice(16 * j, 16 * j + 16)
            g = PG[k, 0, x, o : o + 16].astype(F32)
            b = PG[k, 1, x, o : o + 16].astype(F32)
            sq = jnp.tanh(LAT[x, sl] * g + b)
            m = BASE[x, sl] * jnp.exp(0.25 * sq)
            M[x, sl] = m
            Q[x, sl] = m * 0.25 * (1.0 - sq * sq)
        return 0

    lax.fori_loop(0, 8, model, 0)

    def lap(buf, x, j):
        lo = PAD + T * j
        sl = slice(T * j, T * j + T)
        v = buf[x + 1, lo : lo + T]
        t = CX[x + 1, sl] * (buf[x + 2, lo : lo + T] - v) + CX[x, sl] * (buf[x, lo : lo + T] - v)
        t = t + CY[x, T * j + 1 : T * j + 1 + T] * (buf[x + 1, lo + 1 : lo + 1 + T] - v)
        t = t + CY[x, sl] * (buf[x + 1, lo - 1 : lo - 1 + T] - v)
        zn = jnp.where(lane == 255, 0.0, pltpu.roll(v, 255, 1))
        zp = jnp.where(lane == 0, 0.0, pltpu.roll(v, 1, 1))
        return v, t + CZP[x, sl] * (zn - v) + CZM[x, sl] * (zp - v)

    first = d * 8
    for n in range(4):
        if n > 0:
            h = halo(U.at[n], 1 + n)
            halo_wait(U.at[n], h)
        amp = wav[picked, n]

        def step(x, _):
            factor = jnp.where(first + x == cell_x, amp, 0.0)
            for j in range(16):
                sl = slice(T * j, T * j + T)
                lo = PAD + T * j
                v, a = lap(U.at[n], x, j)
                LU[n, x, sl] = a
                prev = SB[x, sl] if n == 0 else U[n - 1, x + 1, lo : lo + T]
                new = 2.0 * v - prev + M[x, sl] * a + factor * HIT[sl]
                if n < 3:
                    U[n + 1, x + 1, lo : lo + T] = new
                else:
                    U5[x, sl] = new
            return 0

        lax.fori_loop(0, 8, step, 0)
        if n == 0:
            for cp in r_y:
                cp.wait()
            for k in range(2):
                sl = pl.ds(8 * k, 8)
                RZ[k] = RY[gy, sl] + RY[4, sl] + RY[5, sl] + RY[6, sl]
            r_z = rcopy(RZ.at[1 - gz], RZ.at[2], rs.at[6], rr.at[6], zs)
            r_z.start()
        if n == 1:
            r_z.wait()
            RALL[s] = RZ[gz] + RZ[2]
            r_s = []
            for i, p in enumerate((core, zlo, far)):
                cp = rcopy(RALL.at[s], RALL.at[s], rs.at[7 + i], rr.at[7 + i], p)
                cp.start()
                r_s.append(cp)
        if n == 2:
            for cp in r_s:
                cp.wait()
            rt = jnp.transpose(jnp.concatenate([RALL[k] for k in range(4)] + [jnp.zeros((96, 128), F32)], axis=0))
            for k in range(4):
                for x in range(8):
                    RB[k, x] = jnp.broadcast_to(rt[:, 8 * k + x : 8 * k + x + 1], (128, 128))

    for i, n in enumerate((3, 2, 1, 0)):
        if i > 0:
            h = halo(W.at[i - 1], 4 + i)
            halo_wait(W.at[i - 1], h)

        def back(x, _):
            for j in range(16):
                sl = slice(T * j, T * j + T)
                lo = PAD + T * j
                dd = DB[x, sl]
                rr_ = RB[n, x, sl]
                dd = jnp.concatenate([dd, dd], axis=1)
                rr_ = jnp.concatenate([rr_, rr_], axis=1)
                u = U5[x, sl] if n == 3 else U[n + 1, x + 1, lo : lo + T]
                a = jnp.where(lane_f == dd, u - rr_, 0.0)
                if i > 0:
                    _, t = lap(W.at[i - 1], x, j)
                    a = a + t + 2.0 * AA[(i - 1) % 3, x, sl]
                if i > 1:
                    a = a - AA[(i - 2) % 3, x, sl]
                img = a * LU[n, x, sl]
                if i > 0:
                    img = img + IMG[x, sl]
                IMG[x, sl] = img
                if i < 3:
                    AA[i % 3, x, sl] = a
                    W[i, x + 1, lo : lo + T] = M[x, sl] * a
                else:
                    com = img * Q[x, sl]
                    k, o = j // 4, (j % 4) * 8
                    CG[k, 1, x, o : o + 8] = com
                    CG[k, 0, x, o : o + 8] = com * LAT[x, sl]
            return 0

        lax.fori_loop(0, 8, back, 0)

    out_i = load(0, IMG, img_h)

    g_c = []
    for i in range(2):
        cp = rcopy(CG.at[2 * i + (1 - c)], RA.at[i], gs.at[i], gr.at[i], core)
        cp.start()
        g_c.append(cp)

    def add(dst, src):
        def body(x, _):
            for f in range(2):
                dst[f, x] = dst[f, x] + src[f, x]
            return 0

        lax.fori_loop(0, 8, body, 0)

    for cp in g_c:
        cp.wait()
    add(CG.at[2 * (1 - zl) + c], RA.at[1 - zl])
    g_z = rcopy(CG.at[2 * (1 - zl) + c], RBUF, gs.at[2], gr.at[2], zlo)
    g_z.start()
    add(CG.at[s], RA.at[zl])
    g_z.wait()
    add(CG.at[s], RBUF)
    out_g = load(1, CG.at[s, 0], gg_h)
    out_b = load(2, CG.at[s, 1], bg_h)
    out_i.wait()
    out_g.wait()
    out_b.wait()


def shards(
    state_before, state_now, base_model, buoyancy, latent, flow_gain, flow_bias, records, source_wavelet, source_cell,
    shot, receiver_depth,
):
    any_ = pl.BlockSpec(memory_space=pl.ANY)
    smem = pl.BlockSpec(memory_space=pltpu.SMEM)
    vmem = pl.BlockSpec(memory_space=pltpu.VMEM)
    field = (8, 128, 256)
    halo = (10, 144, 256)
    img, gg, bg = pl.pallas_call(
        kernel,
        out_shape=(
            jax.ShapeDtypeStruct(field, F32),
            jax.ShapeDtypeStruct((8, 32, 256), F32),
            jax.ShapeDtypeStruct((8, 32, 256), F32),
        ),
        in_specs=[any_] * 8 + [smem] * 3 + [vmem],
        out_specs=(any_, any_, any_),
        scratch_shapes=[
            pltpu.VMEM((4,) + halo, F32),
            pltpu.VMEM((3,) + halo, F32),
            pltpu.VMEM(halo, F32),
            pltpu.VMEM(field, F32),
            pltpu.VMEM(field, F32),
            pltpu.VMEM(field, F32),
            pltpu.VMEM((4, 2, 8, 32, 256), jnp.bfloat16),
            pltpu.VMEM((2, 256, 128), jnp.bfloat16),
            pltpu.VMEM((4,) + field, F32),
            pltpu.VMEM(field, F32),
            pltpu.VMEM(field, F32),
            pltpu.VMEM(field, F32),
            pltpu.VMEM((9, 128, 256), F32),
            pltpu.VMEM((8, 136, 256), F32),
            pltpu.VMEM(field, F32),
            pltpu.VMEM(field, F32),
            pltpu.VMEM((8, 128, 128), F32),
            pltpu.VMEM((4, 8, 128, 128), F32),
            pltpu.VMEM((128, 256), F32),
            pltpu.VMEM((3,) + field, F32),
            pltpu.VMEM(field, F32),
            pltpu.VMEM((4, 2, 8, 32, 256), F32),
            pltpu.VMEM((2, 2, 8, 32, 256), F32),
            pltpu.VMEM((2, 8, 32, 256), F32),
            pltpu.VMEM((7, 64, 128), F32),
            pltpu.VMEM((7, 16, 128), F32),
            pltpu.VMEM((3, 8, 128), F32),
            pltpu.VMEM((1, 8, 128), F32),
            pltpu.VMEM((4, 8, 128), F32),
            pltpu.SemaphoreType.DMA((8,)),
            pltpu.SemaphoreType.REGULAR,
            pltpu.SemaphoreType.DMA((8, 2)),
            pltpu.SemaphoreType.DMA((8, 2)),
            pltpu.SemaphoreType.DMA((3,)),
            pltpu.SemaphoreType.DMA((3,)),
            pltpu.SemaphoreType.DMA((3,)),
            pltpu.SemaphoreType.DMA((3,)),
            pltpu.SemaphoreType.DMA((10,)),
            pltpu.SemaphoreType.DMA((10,)),
        ],
        compiler_params=pltpu.CompilerParams(
            collective_id=1, has_side_effects=True, vmem_limit_bytes=58 << 20
        ),
        name="flow_gradient",
    )(
        state_before[0], state_now[0], base_model, buoyancy, latent[0], flow_gain, flow_bias, records, source_wavelet,
        source_cell, shot, receiver_depth,
    )
    return img[None], gg, bg


def solution(mesh):
    in_specs = (
        P("smp", "dom", None, None),
        P("smp", "dom", None, None),
        P("dom", None, None),
        P("dom", None, None),
        P("smp", "dom", None, None),
        P("dom", "smp", None),
        P("dom", "smp", None),
        P("dom", None, None, None),
        P(),
        P(),
        P(),
        P("dom", None),
    )
    out_specs = (P("smp", "dom", None, None), P("dom", "smp", None), P("dom", "smp", None))
    return jax.shard_map(shards, mesh=mesh, in_specs=in_specs, out_specs=out_specs, check_vma=False)
```

```python
import functools

import jax
import jax.numpy as jnp
import numpy as np
from jax import lax
from jax.experimental import pallas as pl
from jax.experimental.pallas import tpu as pltpu
from jax.sharding import PartitionSpec as P

MESH = pl.DeviceIdType.MESH
I32 = jnp.int32


def ball(radius):
    return [(a, b) for a in range(-radius, radius + 1) for b in range(abs(a) - radius, radius - abs(a) + 1)]


def near(plane):
    return [(plane + a, y, z) for a in range(-3, 4) for y, z in ball(3 - abs(a))]


def tables():
    lists = [near(x) for x in range(8)]
    pick = np.zeros((128, 64 * len(lists)), np.float32)
    shift = np.zeros((8, 64 * len(lists)), np.float32)
    for i, cells in enumerate(lists):
        cells = cells + [cells[0]] * (64 - len(cells))
        for j, (p, y, z) in enumerate(cells):
            pick[16 * (y + 3) + p + 3, 64 * i + j] = 1.0
            shift[:, 64 * i + j] = z
    return pick, shift
F32 = jnp.float32
PAD = 8
T = 8


def kernel(
    sb_h, sn_h, base_h, buoy_h, lat_h, gain_h, bias_h, rec_h, wav, cell, shot, depth, pick, shift,
    img_h, gg_h, bg_h,
    U, W, B, SB, BASE, LAT, PG, RQ, LU, U5, M, Q, CX, CY, CZP, CZM, DB, RB, HIT, AA, IMG, CA, CB, GA, GB, CG, RA, RBUF, RX, RY, RZ, RS, RALL, DS, DH, IDX, INV,
    lsem, bar_dummy, hs, hr, ps, pr, gs, gr, rs, rr, ds_, dr_,
):
    d = lax.axis_index("dom")
    s = lax.axis_index("smp")
    gx, gy, gz = d // 8, (d // 2) % 4, d % 2
    zl, c = s // 2, s % 2
    left, right = ((d + 31) % 32, s), ((d + 1) % 32, s)
    core = (d, 2 * zl + (1 - c))
    zlo = (d, 2 * (1 - zl) + c)
    far = (d, 2 * (1 - zl) + (1 - c))
    xs = [(((gx + k) % 4) * 8 + d % 8, s) for k in (1, 2, 3)]
    ys = [(gx * 8 + ((gy + k) % 4) * 2 + gz, s) for k in (1, 2, 3)]
    zs = (d - gz + (1 - gz), s)

    def load(i, src, dst):
        cp = pltpu.make_async_copy(src, dst, lsem.at[i])
        cp.start()
        return cp

    rows = pl.ds(PAD, 128)
    inner = pl.ds(1, 8)
    ld_u = load(0, sn_h, U.at[0, inner, rows])
    ld_b = load(1, buoy_h, B.at[inner, rows])
    ld_g = load(2, gain_h, PG.at[s, 0])
    ld_c = load(3, bias_h, PG.at[s, 1])
    ld_r = load(4, rec_h.at[:, s], RQ)
    ld_base = load(5, base_h, BASE)
    ld_lat = load(6, lat_h, LAT)
    ld_sb = load(7, sb_h, SB)

    barrier = pltpu.get_barrier_semaphore()
    peers = [left, right, core, zlo, far] + xs + ys
    for p in peers:
        pl.semaphore_signal(barrier, inc=1, device_id=p, device_id_type=MESH)

    zero = jnp.zeros((T, 256), F32)

    def clear(i, _):
        for n in range(4):
            U[n, i, 0:8] = zero
            U[n, i, 136:144] = zero
        for n in range(3):
            W[n, i, 0:8] = zero
            W[n, i, 136:144] = zero
        B[i, 0:8] = zero
        B[i, 136:144] = zero
        return 0

    lax.fori_loop(0, 10, clear, 0)

    picked = shot[0]
    flat = cell[picked]
    cell_x = flat // (128 * 256)
    cell_y = (flat // 256) % 128
    cell_z = flat % 256
    lane = lax.broadcasted_iota(jnp.int32, (T, 256), 1)
    lane_f = lane.astype(F32)
    sub = lax.broadcasted_iota(jnp.int32, (T, 256), 0)
    for j in range(16):
        HIT[T * j : T * j + T] = jnp.where((sub + T * j == cell_y) & (lane == cell_z), 1.0, 0.0)
    dt = jnp.transpose(jnp.concatenate([depth[...].astype(F32), jnp.zeros((120, 128), F32)], axis=0))
    for x in range(8):
        DB[x] = jnp.broadcast_to(dt[:, x : x + 1], (128, 128))

    pl.semaphore_wait(barrier, len(peers))

    def rcopy(src, dst, ss, sr, dev):
        return pltpu.make_async_remote_copy(
            src_ref=src, dst_ref=dst, send_sem=ss, recv_sem=sr, device_id=dev, device_id_type=MESH
        )

    def halo(buf, i):
        a = rcopy(buf.at[8, rows], buf.at[0, rows], hs.at[i, 0], hr.at[i, 0], right)
        b = rcopy(buf.at[1, rows], buf.at[9, rows], hs.at[i, 1], hr.at[i, 1], left)
        a.start()
        b.start()
        return a, b

    def halo_wait(buf, cps):
        for cp in cps:
            cp.wait()

        @pl.when(d == 0)
        def _():
            for j in range(16):
                buf[0, PAD + T * j : PAD + T * j + T] = zero

        @pl.when(d == 31)
        def _():
            for j in range(16):
                buf[9, PAD + T * j : PAD + T * j + T] = zero

    DS[...] = depth[...].astype(F32)
    d_l = rcopy(DS, DH.at[1], ds_.at[0], dr_.at[0], left)
    d_r = rcopy(DS, DH.at[0], ds_.at[1], dr_.at[1], right)
    d_l.start()
    d_r.start()
    ld_g.wait()
    ld_c.wait()
    p_z = rcopy(PG.at[s], PG.at[s], ps.at[0], pr.at[0], zlo)
    p_c = rcopy(PG.at[s], PG.at[s], ps.at[1], pr.at[1], core)
    p_z.start()
    p_c.start()
    ld_u.wait()
    h_u = halo(U.at[0], 0)
    ld_b.wait()
    h_b = halo(B, 1)

    ld_r.wait()
    mine = (picked // 2 == d).astype(F32)
    odd = (picked % 2).astype(F32)
    for k in range(4):
        r0 = RQ[0, 64 * k : 64 * k + 64].astype(F32)
        r1 = RQ[1, 64 * k : 64 * k + 64].astype(F32)
        RX[k] = (r0 * (1.0 - odd) + r1 * odd) * mine
    r_x = []
    for k in (1, 2, 3):
        cp = rcopy(RX.at[(gx + k) % 4], RX.at[3 + k], rs.at[k - 1], rr.at[k - 1], xs[k - 1])
        cp.start()
        r_x.append(cp)

    ld_base.wait()
    ld_lat.wait()
    ld_sb.wait()

    p_z.wait_recv()
    other = 2 * (1 - zl) + c
    p_f = rcopy(PG.at[other], PG.at[other], ps.at[2], pr.at[2], core)
    p_f.start()
    for cp in h_u:
        cp.wait()
    for cp in h_b:
        cp.wait()

    @pl.when(d == 0)
    def _():
        for j in range(16):
            U[0, 0, PAD + T * j : PAD + T * j + T] = zero
            B[0, PAD + T * j : PAD + T * j + T] = zero

    @pl.when(d == 31)
    def _():
        for j in range(16):
            U[0, 9, PAD + T * j : PAD + T * j + T] = zero
            B[9, PAD + T * j : PAD + T * j + T] = zero

    def coefs(x, _):
        for j in range(17):
            lo = PAD + T * j
            b = B[x + 1, lo : lo + T]
            CY[x, T * j : T * j + T] = 0.5 * (b + B[x + 1, lo - 1 : lo - 1 + T])
            if j < 16:
                CX[x, T * j : T * j + T] = 0.5 * (b + B[x, lo : lo + T])
                zn = jnp.where(lane == 255, 0.0, pltpu.roll(b, 255, 1))
                zp = jnp.where(lane == 0, 0.0, pltpu.roll(b, 1, 1))
                CZP[x, T * j : T * j + T] = 0.5 * (b + zn)
                CZM[x, T * j : T * j + T] = 0.5 * (b + zp)
        return 0

    lax.fori_loop(0, 8, coefs, 0)
    for j in range(16):
        lo = PAD + T * j
        CX[8, T * j : T * j + T] = 0.5 * (B[9, lo : lo + T] + B[8, lo : lo + T])

    r_a = r_x
    for cp in r_a:
        cp.wait()
    for k in range(4):
        sl = pl.ds(16 * k, 16)
        RY[k] = RX[gx, sl] + RX[4, sl] + RX[5, sl] + RX[6, sl]
    r_y = []
    for k in (1, 2, 3):
        cp = rcopy(RY.at[(gy + k) % 4], RY.at[3 + k], rs.at[2 + k], rr.at[2 + k], ys[k - 1])
        cp.start()
        r_y.append(cp)

    d_l.wait()
    d_r.wait()
    near_d = jnp.concatenate([DH[0, 5:8], DS[...], DH[1, 0:3], jnp.zeros((2, 128), F32)], axis=0)
    rolled = [near_d if y == 0 else pltpu.roll(near_d, (-y) % 128, 1) for y in range(-3, 4)]
    key = jnp.transpose(jnp.concatenate(rolled + [jnp.zeros((16, 128), F32)], axis=0)).astype(jnp.bfloat16)
    idx = jnp.dot(key, pick[...], preferred_element_type=F32) + shift[0:1, :]
    idx = jnp.clip(idx, 0.0, 255.0).astype(I32)
    for q in range(4):
        IDX[q] = idx[:, 128 * q : 128 * q + 128]

    def invert(t, _):
        at = pl.ds(pl.multiple_of(32 * s + T * t, T), T)
        for q in range(4):
            tile = IDX[q, at]
            for h in range(2):
                inv = jnp.full((T, 256), -1, I32)
                for j in range(63):
                    jj = 64 * h + j
                    inv = jnp.where(lane == tile[:, jj : jj + 1], jj, inv)
                INV[2 * q + h, t] = inv
        return 0

    lax.fori_loop(0, 4, invert, 0)

    p_c.wait()
    p_f.wait()
    p_z.wait_send()

    def model(x, _):
        for j in range(8):
            k, o = j // 2, (j % 2) * 16
            sl = slice(16 * j, 16 * j + 16)
            g = PG[k, 0, x, o : o + 16].astype(F32)
            b = PG[k, 1, x, o : o + 16].astype(F32)
            sq = jnp.tanh(LAT[x, sl] * g + b)
            m = BASE[x, sl] * jnp.exp(0.25 * sq)
            M[x, sl] = m
            Q[x, sl] = m * 0.25 * (1.0 - sq * sq)
        return 0

    lax.fori_loop(0, 8, model, 0)

    def lap(buf, x, j):
        lo = PAD + T * j
        sl = slice(T * j, T * j + T)
        v = buf[x + 1, lo : lo + T]
        t = CX[x + 1, sl] * (buf[x + 2, lo : lo + T] - v) + CX[x, sl] * (buf[x, lo : lo + T] - v)
        t = t + CY[x, T * j + 1 : T * j + 1 + T] * (buf[x + 1, lo + 1 : lo + 1 + T] - v)
        t = t + CY[x, sl] * (buf[x + 1, lo - 1 : lo - 1 + T] - v)
        zn = jnp.where(lane == 255, 0.0, pltpu.roll(v, 255, 1))
        zp = jnp.where(lane == 0, 0.0, pltpu.roll(v, 1, 1))
        return v, t + CZP[x, sl] * (zn - v) + CZM[x, sl] * (zp - v)

    first = d * 8
    for n in range(4):
        if n > 0:
            h = halo(U.at[n], 1 + n)
            halo_wait(U.at[n], h)
        amp = wav[picked, n]

        def step(x, _):
            factor = jnp.where(first + x == cell_x, amp, 0.0)
            for j in range(16):
                sl = slice(T * j, T * j + T)
                lo = PAD + T * j
                v, a = lap(U.at[n], x, j)
                LU[n, x, sl] = a
                prev = SB[x, sl] if n == 0 else U[n - 1, x + 1, lo : lo + T]
                new = 2.0 * v - prev + M[x, sl] * a + factor * HIT[sl]
                if n < 3:
                    U[n + 1, x + 1, lo : lo + T] = new
                else:
                    U5[x, sl] = new
            return 0

        lax.fori_loop(0, 8, step, 0)
        if n == 0:
            for cp in r_y:
                cp.wait()
            for k in range(2):
                sl = pl.ds(8 * k, 8)
                RZ[k] = RY[gy, sl] + RY[4, sl] + RY[5, sl] + RY[6, sl]
            r_z = rcopy(RZ.at[1 - gz], RZ.at[2], rs.at[6], rr.at[6], zs)
            r_z.start()
        if n == 1:
            r_z.wait()
            RALL[s] = RZ[gz] + RZ[2]
            r_s = []
            for i, p in enumerate((core, zlo, far)):
                cp = rcopy(RALL.at[s], RALL.at[s], rs.at[7 + i], rr.at[7 + i], p)
                cp.start()
                r_s.append(cp)
        if n == 2:
            for cp in r_s:
                cp.wait()
            rt = jnp.transpose(jnp.concatenate([RALL[k] for k in range(4)] + [jnp.zeros((96, 128), F32)], axis=0))
            for k in range(4):
                for x in range(8):
                    RB[k, x] = jnp.broadcast_to(rt[:, 8 * k + x : 8 * k + x + 1], (128, 128))

    for i, n in enumerate((3, 2, 1, 0)):
        if i > 0:
            h = halo(W.at[i - 1], 4 + i)
            halo_wait(W.at[i - 1], h)

        def back(x, _):
            for j in range(16):
                sl = slice(T * j, T * j + T)
                lo = PAD + T * j
                dd = DB[x, sl]
                rr_ = RB[n, x, sl]
                dd = jnp.concatenate([dd, dd], axis=1)
                rr_ = jnp.concatenate([rr_, rr_], axis=1)
                u = U5[x, sl] if n == 3 else U[n + 1, x + 1, lo : lo + T]
                a = jnp.where(lane_f == dd, u - rr_, 0.0)
                if i > 0:
                    _, t = lap(W.at[i - 1], x, j)
                    a = a + t + 2.0 * AA[(i - 1) % 3, x, sl]
                if i > 1:
                    a = a - AA[(i - 2) % 3, x, sl]
                img = a * LU[n, x, sl]
                if i > 0:
                    img = img + IMG[x, sl]
                IMG[x, sl] = img
                if i < 3:
                    AA[i % 3, x, sl] = a
                    W[i, x + 1, lo : lo + T] = M[x, sl] * a
                else:
                    com = img * Q[x, sl]
                    CB[x, sl] = com
                    CA[x, sl] = com * LAT[x, sl]
            return 0

        lax.fori_loop(0, 8, back, 0)

    out_i = load(0, IMG, img_h)

    lane1 = lax.broadcasted_iota(I32, (T, 128), 1)

    def compact(k):
        def body(t, _):
            at = pl.ds(pl.multiple_of(32 * k + T * t, T), T)
            for q in range(4):
                tile = IDX[q, at]
                low, tile = tile < 128, tile & 127
                for f, src in enumerate((CA, CB)):
                    halves = []
                    for x in (2 * q, 2 * q + 1):
                        v = src[x, at]
                        g0 = jnp.take_along_axis(v[:, :128], tile, axis=1, mode="promise_in_bounds")
                        g1 = jnp.take_along_axis(v[:, 128:], tile, axis=1, mode="promise_in_bounds")
                        halves.append(jnp.where(low, g0, g1))
                    CG[k, f, q, t] = jnp.where(lane1 < 64, halves[0], halves[1])
            return 0

        lax.fori_loop(0, 4, body, 0)

    g_c = []
    for i in (1 - zl, zl):
        compact(2 * i + (1 - c))
        cp = rcopy(CG.at[2 * i + (1 - c)], RA.at[i], gs.at[i], gr.at[i], core)
        cp.start()
        g_c.append(cp)
    pair = 2 * (1 - zl) + c
    compact(pair)
    g_c[0].wait()
    for f in range(2):
        for q in range(4):
            CG[pair, f, q] = CG[pair, f, q] + RA[1 - zl, f, q]
    g_z = rcopy(CG.at[pair], RBUF, gs.at[2], gr.at[2], zlo)
    g_z.start()
    g_c[1].wait()
    g_z.wait()

    def spread(t, _):
        at = pl.ds(pl.multiple_of(32 * s + T * t, T), T)
        to = pl.ds(pl.multiple_of(T * t, T), T)
        for q in range(4):
            for f, src, out in ((0, CA, GA), (1, CB, GB)):
                v = RA[zl, f, q, t] + RBUF[f, q, t]
                for x in (2 * q, 2 * q + 1):
                    inv = INV[x, t]
                    have, inv = inv >= 0, inv & 127
                    g0 = jnp.take_along_axis(v, inv[:, :128], axis=1, mode="promise_in_bounds")
                    g1 = jnp.take_along_axis(v, inv[:, 128:], axis=1, mode="promise_in_bounds")
                    g = jnp.concatenate([g0, g1], axis=1)
                    out[x, to] = src[x, at] + jnp.where(have, g, 0.0)
        return 0

    lax.fori_loop(0, 4, spread, 0)
    out_g = load(1, GA, gg_h)
    out_b = load(2, GB, bg_h)
    out_i.wait()
    out_g.wait()
    out_b.wait()


def shards(
    state_before, state_now, base_model, buoyancy, latent, flow_gain, flow_bias, records, source_wavelet, source_cell,
    shot, receiver_depth,
):
    any_ = pl.BlockSpec(memory_space=pl.ANY)
    smem = pl.BlockSpec(memory_space=pltpu.SMEM)
    vmem = pl.BlockSpec(memory_space=pltpu.VMEM)
    field = (8, 128, 256)
    halo = (10, 144, 256)
    pick, shift = tables()
    img, gg, bg = pl.pallas_call(
        kernel,
        out_shape=(
            jax.ShapeDtypeStruct(field, F32),
            jax.ShapeDtypeStruct((8, 32, 256), F32),
            jax.ShapeDtypeStruct((8, 32, 256), F32),
        ),
        in_specs=[any_] * 8 + [smem] * 3 + [vmem] * 3,
        out_specs=(any_, any_, any_),
        scratch_shapes=[
            pltpu.VMEM((4,) + halo, F32),
            pltpu.VMEM((3,) + halo, F32),
            pltpu.VMEM(halo, F32),
            pltpu.VMEM(field, F32),
            pltpu.VMEM(field, F32),
            pltpu.VMEM(field, F32),
            pltpu.VMEM((4, 2, 8, 32, 256), jnp.bfloat16),
            pltpu.VMEM((2, 256, 128), jnp.bfloat16),
            pltpu.VMEM((4,) + field, F32),
            pltpu.VMEM(field, F32),
            pltpu.VMEM(field, F32),
            pltpu.VMEM(field, F32),
            pltpu.VMEM((9, 128, 256), F32),
            pltpu.VMEM((8, 136, 256), F32),
            pltpu.VMEM(field, F32),
            pltpu.VMEM(field, F32),
            pltpu.VMEM((8, 128, 128), F32),
            pltpu.VMEM((4, 8, 128, 128), F32),
            pltpu.VMEM((128, 256), F32),
            pltpu.VMEM((3,) + field, F32),
            pltpu.VMEM(field, F32),
            pltpu.VMEM(field, F32),
            pltpu.VMEM(field, F32),
            pltpu.VMEM((8, 32, 256), F32),
            pltpu.VMEM((8, 32, 256), F32),
            pltpu.VMEM((4, 2, 4, 4, 8, 128), F32),
            pltpu.VMEM((2, 2, 4, 4, 8, 128), F32),
            pltpu.VMEM((2, 4, 4, 8, 128), F32),
            pltpu.VMEM((7, 64, 128), F32),
            pltpu.VMEM((7, 16, 128), F32),
            pltpu.VMEM((3, 8, 128), F32),
            pltpu.VMEM((1, 8, 128), F32),
            pltpu.VMEM((4, 8, 128), F32),
            pltpu.VMEM((8, 128), F32),
            pltpu.VMEM((2, 8, 128), F32),
            pltpu.VMEM((4, 128, 128), I32),
            pltpu.VMEM((8, 4, 8, 256), I32),
            pltpu.SemaphoreType.DMA((8,)),
            pltpu.SemaphoreType.REGULAR,
            pltpu.SemaphoreType.DMA((8, 2)),
            pltpu.SemaphoreType.DMA((8, 2)),
            pltpu.SemaphoreType.DMA((3,)),
            pltpu.SemaphoreType.DMA((3,)),
            pltpu.SemaphoreType.DMA((3,)),
            pltpu.SemaphoreType.DMA((3,)),
            pltpu.SemaphoreType.DMA((10,)),
            pltpu.SemaphoreType.DMA((10,)),
            pltpu.SemaphoreType.DMA((2,)),
            pltpu.SemaphoreType.DMA((2,)),
        ],
        compiler_params=pltpu.CompilerParams(
            collective_id=1, has_side_effects=True, vmem_limit_bytes=58 << 20
        ),
        name="flow_gradient",
    )(
        state_before[0], state_now[0], base_model, buoyancy, latent[0], flow_gain, flow_bias, records, source_wavelet,
        source_cell, shot, receiver_depth, jnp.asarray(pick, jnp.bfloat16), jnp.asarray(shift),
    )
    return img[None], gg, bg


def solution(mesh):
    in_specs = (
        P("smp", "dom", None, None),
        P("smp", "dom", None, None),
        P("dom", None, None),
        P("dom", None, None),
        P("smp", "dom", None, None),
        P("dom", "smp", None),
        P("dom", "smp", None),
        P("dom", None, None, None),
        P(),
        P(),
        P(),
        P("dom", None),
    )
    out_specs = (P("smp", "dom", None, None), P("dom", "smp", None), P("dom", "smp", None))
    return jax.shard_map(shards, mesh=mesh, in_specs=in_specs, out_specs=out_specs, check_vma=False)
```

```python
import functools

import jax
import jax.numpy as jnp
import numpy as np
from jax import lax
from jax.experimental import pallas as pl
from jax.experimental.pallas import tpu as pltpu
from jax.sharding import PartitionSpec as P

MESH = pl.DeviceIdType.MESH
I32 = jnp.int32


def ball(radius):
    return [(a, b) for a in range(-radius, radius + 1) for b in range(abs(a) - radius, radius - abs(a) + 1)]


def near(plane):
    return [(plane + a, y, z) for a in range(-3, 4) for y, z in ball(3 - abs(a))]


def across(height):
    radius = {1: {0: 2, -1: 2, 1: 1, -2: 1, 2: 0, -3: 0}, 2: {0: 1, -1: 1, -2: 1, 1: 0, -3: 0}, 3: {0: 0, -2: 0, -3: 0}}
    return [(p, y, z) for p, r in radius[height].items() for y, z in ball(r)]


COUNTS = [len(across(h)) for h in (1, 2, 3)]
STARTS = [sum(COUNTS[:h]) for h in range(4)]


SPARE = 58
USCALE = 32767.0 / 6.0
BSCALE = 65532.0


def tables():
    up = sum((across(h) for h in (1, 2, 3)), [])
    down = [(-1 - p, y, z) for p, y, z in up]
    right = [[(p + 8, y, z) for p, y, z in cells] for cells in (up, down)]
    lists = [near(x) for x in range(8)] + [down, right[0], up, right[1]]
    pick = np.zeros((128, 64 * len(lists)), np.float32)
    shift = np.zeros((8, 64 * len(lists)), np.float32)
    for i, cells in enumerate(lists):
        if i >= 8:
            cells = cells + [{8: (-1, 0, 0), 9: (8, 0, 0), 10: (0, 0, 0), 11: (7, 0, 0)}[i]]
        cells = cells + [cells[0]] * (64 - len(cells))
        for j, (p, y, z) in enumerate(cells):
            pick[16 * (y + 3) + p + 3, 64 * i + j] = 1.0
            shift[:, 64 * i + j] = z
    return pick, shift


F32 = jnp.float32
PAD = 8
T = 8


def kernel(
    sb_h, sn_h, base_h, buoy_h, lat_h, gain_h, bias_h, rec_h, wav, cell, shot, depth, pick, shift,
    img_h, gg_h, bg_h,
    U, B, SB, BASE, LAT, PG, RQ, LU, AA, M, Q, CX, CY, CZP, CZM, DB, RB, HIT, IMG, CA, CB, GA, GB, CG, RA, RBUF,
    RX, RY, RZ, RALL, DS, DH, IDX, INV, SIDX, RIDX, INVH, SE, RE, SG, RG, KT, SR, RR,
    lsem, es, er, hs, hr, ps, pr, gs, gr, rs, rr, ds_, dr_,
):
    d = lax.axis_index("dom")
    s = lax.axis_index("smp")
    gx, gy, gz = d // 8, (d // 2) % 4, d % 2
    zl, c = s // 2, s % 2
    left, right = ((d + 31) % 32, s), ((d + 1) % 32, s)
    core = (d, 2 * zl + (1 - c))
    zlo = (d, 2 * (1 - zl) + c)
    far = (d, 2 * (1 - zl) + (1 - c))
    xs = [(((gx + k) % 4) * 8 + d % 8, s) for k in (1, 2, 3)]
    ys = [(gx * 8 + ((gy + k) % 4) * 2 + gz, s) for k in (1, 2, 3)]
    zs = (d - gz + (1 - gz), s)

    def load(i, src, dst):
        cp = pltpu.make_async_copy(src, dst, lsem.at[i])
        cp.start()
        return cp

    rows = pl.ds(PAD, 128)
    own = pl.ds(3, 8)
    ld_g = load(2, gain_h, PG.at[s, 0])
    ld_c = load(3, bias_h, PG.at[s, 1])
    ld_u = load(0, sn_h, U.at[0, own, rows])
    ld_b = load(1, buoy_h, B.at[own, rows])
    ld_r = load(4, rec_h.at[:, s], RQ)
    ld_base = load(5, base_h, BASE)
    ld_lat = load(6, lat_h, LAT)
    ld_sb = load(7, sb_h, SB)

    barrier = pltpu.get_barrier_semaphore()
    peers = [left, right, core, zlo, far] + xs + ys
    for p in peers:
        pl.semaphore_signal(barrier, inc=1, device_id=p, device_id_type=MESH)

    def rcopy(src, dst, ss, sr, dev):
        return pltpu.make_async_remote_copy(
            src_ref=src, dst_ref=dst, send_sem=ss, recv_sem=sr, device_id=dev, device_id_type=MESH
        )

    def loop(n, body):
        def run(i, _):
            body(i)
            return 0

        lax.fori_loop(0, n, run, 0)

    zero = jnp.zeros((T, 256), F32)
    lane = lax.broadcasted_iota(I32, (T, 256), 1)
    lane1 = lax.broadcasted_iota(I32, (T, 128), 1)
    lane_f = lane.astype(F32)

    def tile(j):
        return slice(T * j, T * j + T)

    def padded(j):
        return slice(PAD + T * j, PAD + T * j + T)

    def twice(v):
        return jnp.concatenate([v, v], axis=1)

    def clear(i):
        for n in range(4):
            U[n, i, 0:8] = zero
            U[n, i, 136:144] = zero
        B[i, 0:8] = zero
        B[i, 136:144] = zero
        for j in range(16):
            AA[4, i, tile(j)] = zero

    loop(14, clear)

    picked = shot[0]
    flat = cell[picked]
    cell_x = flat // (128 * 256)
    cell_y = (flat // 256) % 128
    cell_z = flat % 256
    sub = lax.broadcasted_iota(I32, (T, 256), 0)
    for j in range(16):
        HIT[tile(j)] = jnp.where((sub + T * j == cell_y) & (lane == cell_z), 1.0, 0.0)
    DS[...] = depth[...].astype(F32)

    ld_u.wait()
    ld_b.wait()
    for e, p in enumerate((0, 7)):
        for j in range(8):
            sl = slice(16 * j, 16 * j + 16)
            at = slice(PAD + 16 * j, PAD + 16 * j + 16)
            SE[e, 0, sl] = jnp.round(U[0, p + 3, at] * USCALE).astype(I32).astype(jnp.int16)
            SE[e, 1, sl] = jnp.round((B[p + 3, at] - 1.0) * BSCALE).astype(I32).astype(jnp.int16)

    ld_g.wait()
    ld_c.wait()
    pl.semaphore_wait(barrier, len(peers))

    d_l = rcopy(DS, DH.at[1], ds_.at[0], dr_.at[0], left)
    d_r = rcopy(DS, DH.at[0], ds_.at[1], dr_.at[1], right)
    d_l.start()
    d_r.start()
    p_z = rcopy(PG.at[s], PG.at[s], ps.at[0], pr.at[0], zlo)
    p_c = rcopy(PG.at[s], PG.at[s], ps.at[1], pr.at[1], core)
    e_l = rcopy(SE.at[0], RE.at[1], es.at[0], er.at[0], left)
    e_r = rcopy(SE.at[1], RE.at[0], es.at[1], er.at[1], right)
    e_l.start()
    e_r.start()
    p_z.start()
    p_c.start()

    ld_r.wait()
    mine = (picked // 2 == d).astype(F32)
    odd = (picked % 2).astype(F32)
    for k in range(4):
        r0 = RQ[0, 64 * k : 64 * k + 64].astype(F32)
        r1 = RQ[1, 64 * k : 64 * k + 64].astype(F32)
        RX[k] = (r0 * (1.0 - odd) + r1 * odd) * mine
    r_x = []
    for k in (1, 2, 3):
        cp = rcopy(RX.at[(gx + k) % 4], RX.at[3 + k], rs.at[k - 1], rr.at[k - 1], xs[k - 1])
        cp.start()
        r_x.append(cp)

    def coef_yz(p):
        for j in range(17):
            lo = PAD + T * j
            b = B[p + 3, lo : lo + T]
            CY[p + 2, tile(j)] = 0.5 * (b + B[p + 3, lo - 1 : lo - 1 + T])
            if j < 16:
                zn = jnp.where(lane == 255, 0.0, pltpu.roll(b, 255, 1))
                zp = jnp.where(lane == 0, 0.0, pltpu.roll(b, 1, 1))
                CZP[p + 2, tile(j)] = 0.5 * (b + zn)
                CZM[p + 2, tile(j)] = 0.5 * (b + zp)

    def coef_x(p):
        for j in range(16):
            CX[p + 3, tile(j)] = 0.5 * (B[p + 3, padded(j)] + B[p + 4, padded(j)])

    loop(8, coef_yz)
    loop(7, coef_x)

    def lap(k, p, j):
        lo = PAD + T * j
        sl = tile(j)
        v = U[k, p + 3, lo : lo + T]
        t = CX[p + 3, sl] * (U[k, p + 4, lo : lo + T] - v) + CX[p + 2, sl] * (U[k, p + 2, lo : lo + T] - v)
        t = t + CY[p + 2, T * j + 1 : T * j + 1 + T] * (U[k, p + 3, lo + 1 : lo + 1 + T] - v)
        t = t + CY[p + 2, sl] * (U[k, p + 3, lo - 1 : lo - 1 + T] - v)
        zn = jnp.where(lane == 255, 0.0, pltpu.roll(v, 255, 1))
        zp = jnp.where(lane == 0, 0.0, pltpu.roll(v, 1, 1))
        return v, t + CZP[p + 2, sl] * (zn - v) + CZM[p + 2, sl] * (zp - v)

    def first_lap(p):
        for j in range(16):
            LU[0, p + 3, tile(j)] = lap(0, p, j)[1]

    loop(6, lambda i: first_lap(i + 1))

    d_l.wait()
    d_r.wait()
    near_d = jnp.concatenate([DH[0, 5:8], DS[...], DH[1, 0:3], jnp.zeros((2, 128), F32)], axis=0)
    rolled = [near_d if y == 0 else pltpu.roll(near_d, (-y) % 128, 1) for y in range(-3, 4)]
    key = jnp.transpose(jnp.concatenate(rolled + [jnp.zeros((16, 128), F32)], axis=0))
    for p in range(14):
        DB[p] = jnp.broadcast_to(key[:, 48 + p : 49 + p], (128, 128))
    idx = jnp.dot(key.astype(jnp.bfloat16), pick[...], preferred_element_type=F32) + shift[0:1, :]
    idx = jnp.clip(idx, 0.0, 255.0).astype(I32)
    for q in range(4):
        IDX[q] = idx[:, 128 * q : 128 * q + 128]
    SIDX[...] = idx[:, 512:640]
    RIDX[...] = idx[:, 640:768]

    def take(v, i):
        return jnp.take_along_axis(v, i, axis=1, mode="promise_in_bounds")

    def compact(which, read, spare=None):
        def body(t):
            halves = []
            for half in range(2):
                i = SIDX[pl.ds(pl.multiple_of(64 * half + T * t, T), T)]
                low, i = i < 128, i & 127
                for side in range(2):
                    for h in range(3):
                        v = read(7 - h if side else h, 64 * half + T * t)
                        g = jnp.where(low, take(v[:, :128], i), take(v[:, 128:], i))
                        start = 64 * side + STARTS[h]
                        out = g if start == 0 else jnp.where(lane1 >= start, g, out)
                    if spare is not None:
                        v = spare(6 if side else 1, 64 * half + T * t)
                        g = jnp.where(low, take(v[:, :128], i), take(v[:, 128:], i))
                        out = jnp.where(lane1 == 64 * side + SPARE, g, out)
                halves.append(out)
            a, b = halves
            SG[which, 0, t] = jnp.where(lane1 < 64, a, pltpu.roll(b, 64, 1))
            SG[which, 1, t] = jnp.where(lane1 < 64, pltpu.roll(a, 64, 1), b)

        loop(8, body)
        a = rcopy(SG.at[which, 0], RG.at[which, 1], hs.at[which, 0], hr.at[which, 0], left)
        b = rcopy(SG.at[which, 1], RG.at[which, 0], hs.at[which, 1], hr.at[which, 1], right)
        a.start()
        b.start()
        return a, b

    def at_ends(do):
        @pl.when(d == 0)
        def _():
            do(0)

        @pl.when(d == 31)
        def _():
            do(1)

    def expand(which, cps, write, heights):
        for cp in cps:
            cp.wait()

        def blank(side):
            for t in range(8):
                RG[which, side, t] = jnp.zeros((T, 128), F32)

        at_ends(blank)

        def body(t):
            for side in range(2):
                v = RG[which, side, t % 8]
                for h in heights:
                    i = INVH[3 * side + h, t]
                    g = jnp.concatenate([take(v, i[:, :128]), take(v, i[:, 128:])], axis=1)
                    write(8 + h if side else -1 - h, T * t, g)

        loop(16, body)

    def rows_at(first, n=T):
        return pl.ds(pl.multiple_of(first, T), n)

    h_b = compact(0, lambda p, y: B[p + 3, rows_at(PAD + y)])

    def invert_halo(t):
        cells = RIDX[rows_at(T * t)]
        for side in range(2):
            for h in range(3):
                inv = jnp.zeros((T, 256), I32)
                for j in range(STARTS[h], STARTS[h + 1]):
                    jj = 64 * side + j
                    inv = jnp.where(lane == cells[:, jj : jj + 1], j, inv)
                INVH[3 * side + h, t] = inv + 64 * (t // 8)

    loop(16, invert_halo)

    p_z.wait_recv()
    other = 2 * (1 - zl) + c
    p_f = rcopy(PG.at[other], PG.at[other], ps.at[2], pr.at[2], core)
    p_f.start()

    for cp in r_x:
        cp.wait()
    for k in range(4):
        sl = pl.ds(16 * k, 16)
        RY[k] = RX[gx, sl] + RX[4, sl] + RX[5, sl] + RX[6, sl]
    r_y = []
    for k in (1, 2, 3):
        cp = rcopy(RY.at[(gy + k) % 4], RY.at[3 + k], rs.at[2 + k], rr.at[2 + k], ys[k - 1])
        cp.start()
        r_y.append(cp)

    e_l.wait()
    e_r.wait()
    for e, p in enumerate((-1, 8)):
        for j in range(8):
            sl = slice(16 * j, 16 * j + 16)
            at = slice(PAD + 16 * j, PAD + 16 * j + 16)
            U[0, p + 3, at] = RE[e, 0, sl].astype(I32).astype(F32) * (1.0 / USCALE)
            B[p + 3, at] = RE[e, 1, sl].astype(I32).astype(F32) * (1.0 / BSCALE) + 1.0

    def no_edge(side):
        for j in range(16):
            U[0, 11 if side else 2, padded(j)] = zero
            B[11 if side else 2, padded(j)] = zero

    at_ends(no_edge)
    loop(2, lambda i: coef_x(8 * i - 1))
    loop(2, lambda i: first_lap(7 * i))
    ld_base.wait()
    ld_lat.wait()
    ld_sb.wait()
    p_c.wait()
    p_f.wait()
    p_z.wait_send()

    first = d * 8

    def step_one(p):
        factor = jnp.where(first + p == cell_x, wav[picked, 0], 0.0)
        for j in range(8):
            k, o = j // 2, (j % 2) * 16
            sl = slice(16 * j, 16 * j + 16)
            at = slice(PAD + 16 * j, PAD + 16 * j + 16)
            g = PG[k, 0, p, o : o + 16].astype(F32)
            b = PG[k, 1, p, o : o + 16].astype(F32)
            sq = jnp.tanh(LAT[p, sl] * g + b)
            m = BASE[p, sl] * jnp.exp(0.25 * sq)
            M[p + 3, sl] = m
            Q[p, sl] = m * 0.25 * (1.0 - sq * sq)
            U[1, p + 3, at] = 2.0 * U[0, p + 3, at] - SB[p, sl] + m * LU[0, p + 3, sl] + factor * HIT[sl]

    loop(6, lambda i: step_one(i + 2 * (i // 3)))
    h_u = compact(1, lambda p, y: U[1, p + 3, rows_at(PAD + y)], lambda p, y: U[0, p + 3, rows_at(PAD + y)])
    h_m = compact(2, lambda p, y: M[p + 3, rows_at(y)])
    loop(2, lambda i: step_one(i + 3))

    for cp in r_y:
        cp.wait()
    for k in range(2):
        sl = pl.ds(8 * k, 8)
        RZ[k] = RY[gy, sl] + RY[4, sl] + RY[5, sl] + RY[6, sl]
    r_z = rcopy(RZ.at[1 - gz], RZ.at[2], rs.at[6], rr.at[6], zs)
    r_z.start()

    def write_b(p, y, g):
        B[p + 3, rows_at(PAD + y)] = g

    expand(0, h_b, write_b, (1, 2))
    loop(2, lambda i: coef_yz(9 * i - 1))
    loop(2, lambda i: coef_yz(11 * i - 2))
    loop(2, lambda i: coef_x(10 * i - 2))
    loop(2, lambda i: coef_x(12 * i - 3))

    r_z.wait()
    RALL[s] = RZ[gz] + RZ[2]
    r_s = []
    for i, p in enumerate((core, zlo, far)):
        cp = rcopy(RALL.at[s], RALL.at[s], rs.at[7 + i], rr.at[7 + i], p)
        cp.start()
        r_s.append(cp)

    def step(n, p):
        factor = jnp.where(first + p == cell_x, wav[picked, n], 0.0)
        for j in range(16):
            sl = tile(j)
            v, a = lap(n, p, j)
            LU[n, p + 3, sl] = a
            new = 2.0 * v - U[n - 1, p + 3, padded(j)] + M[p + 3, sl] * a + factor * HIT[sl]
            U[n + 1, p + 3, padded(j)] = new
            AA[n, p + 3, sl] = jnp.where(lane_f == twice(DB[p + 3, sl]), new - twice(RB[n, p + 3, sl]), 0.0)

    def last_step(p):
        factor = jnp.where(first + p == cell_x, wav[picked, 3], 0.0)
        for j in range(16):
            sl = tile(j)
            v, a = lap(3, p, j)
            m = M[p + 3, sl]
            LU[3, p + 3, sl] = a
            new = 2.0 * v - U[2, p + 3, padded(j)] + m * a + factor * HIT[sl]
            r = jnp.where(lane_f == twice(DB[p + 3, sl]), new - twice(RB[3, p + 3, sl]), 0.0)
            AA[3, p + 3, sl] = r
            U[0, p + 3, padded(j)] = m * r

    for cp in r_s:
        cp.wait()
    rt = jnp.transpose(jnp.concatenate([RALL[k] for k in range(4)] + [jnp.zeros((96, 128), F32)], axis=0))
    for k in range(4):
        for x in range(8):
            RB[k, x + 3] = jnp.broadcast_to(rt[:, 8 * k + x : 8 * k + x + 1], (128, 128))

    def inside(t, _):
        loop(6 - 2 * t, lambda i: step(1 + t, 1 + t + i))
        return 0

    lax.fori_loop(0, 2, inside, 0)
    loop(2, lambda i: last_step(3 + i))

    def write_u(p, y, g):
        U[1, p + 3, rows_at(PAD + y)] = g

    def write_m(p, y, g):
        M[p + 3, rows_at(y)] = g

    expand(1, h_u, write_u, (0, 1, 2))

    def second(t):
        slot = jnp.full((T, 128), SPARE, I32) + 64 * (t // 8)
        for side in range(2):
            U[0, 12 if side else 1, rows_at(PAD + T * t)] = twice(take(RG[1, side, t % 8], slot))

    loop(16, second)
    expand(2, h_m, write_m, (0, 1, 2))

    def outside(t, _):
        loop(6, lambda i: step(1 + t, t - 2 + i + (6 - 2 * t) * (i // 3)))
        return 0

    lax.fori_loop(0, 2, outside, 0)
    loop(6, lambda i: last_step(i + 2 * (i // 3)))

    sends = [(3, 0), (3, 1), (3, 2), (2, 0), (2, 1), (1, 0)]

    def pack(t):
        at = rows_at(T * t)
        out = jnp.zeros((T, 128), F32)
        for side in range(2):
            for i, (k, h) in enumerate(sends):
                total = jnp.sum(AA[k, 3 + (7 - h if side else h), at], axis=1, keepdims=True)
                out = jnp.where(lane1 == 8 * side + i, total, out)
        KT[at] = out

    loop(16, pack)
    packed = jnp.transpose(KT[...])
    SR[0] = packed[0:8]
    SR[1] = packed[8:16]
    r_l = rcopy(SR.at[0], RR.at[1], ds_.at[2], dr_.at[2], left)
    r_r = rcopy(SR.at[1], RR.at[0], ds_.at[3], dr_.at[3], right)
    r_l.start()
    r_r.start()

    def back(k, p):
        for j in range(16):
            sl = tile(j)
            _, t = lap(3 - k, p, j)
            a = AA[k - 1, p + 3, sl] + t + 2.0 * AA[k, p + 3, sl] - AA[k + 1, p + 3, sl]
            AA[k - 1, p + 3, sl] = a
            U[4 - k, p + 3, padded(j)] = M[p + 3, sl] * a

    def finish(p):
        for j in range(16):
            sl = tile(j)
            _, t = lap(2, p, j)
            a2, a3 = AA[1, p + 3, sl], AA[2, p + 3, sl]
            a1 = AA[0, p + 3, sl] + t + 2.0 * a2 - a3
            img = AA[3, p + 3, sl] * LU[3, p + 3, sl] + a3 * LU[2, p + 3, sl]
            img = img + a2 * LU[1, p + 3, sl] + a1 * LU[0, p + 3, sl]
            IMG[p, sl] = img
            com = img * Q[p, sl]
            CB[p, sl] = com
            CA[p, sl] = com * LAT[p, sl]

    def resid_one(p):
        for j in range(16):
            sl = tile(j)
            r = U[1, p + 3, padded(j)] - twice(RB[0, p + 3, sl])
            AA[0, p + 3, sl] = jnp.where(lane_f == twice(DB[p + 3, sl]), r, 0.0)

    loop(8, resid_one)

    def inside_back(t, _):
        loop(6 - 2 * t, lambda i: back(3 - t, 1 + t + i))
        return 0

    lax.fori_loop(0, 2, inside_back, 0)
    loop(2, lambda i: finish(3 + i))

    def invert(t):
        at = rows_at(32 * s + T * t)
        for q in range(4):
            cells = IDX[q, at]
            for h in range(2):
                inv = jnp.full((T, 256), -1, I32)
                for j in range(63):
                    jj = 64 * h + j
                    inv = jnp.where(lane == cells[:, jj : jj + 1], jj, inv)
                INV[2 * q + h, t] = inv

    loop(4, invert)

    r_l.wait()
    r_r.wait()

    def no_resid(side):
        RR[side] = jnp.zeros((8, 128), F32)

    at_ends(no_resid)
    KT[...] = jnp.transpose(jnp.concatenate([RR[0], RR[1], jnp.zeros((112, 128), F32)], axis=0))
    for side in range(2):
        for i, (k, h) in enumerate(sends):
            p = 8 + h if side else -1 - h
            for j in range(16):
                sl = tile(j)
                col = 8 * side + i
                r = jnp.where(lane_f == twice(DB[p + 3, sl]), KT[sl, col : col + 1], 0.0)
                AA[k, p + 3, sl] = r
                if k == 3:
                    U[0, p + 3, padded(j)] = M[p + 3, sl] * r

    def outside_back(t, _):
        loop(6, lambda i: back(3 - t, t - 2 + i + (6 - 2 * t) * (i // 3)))
        return 0

    lax.fori_loop(0, 2, outside_back, 0)
    loop(6, lambda i: finish(i + 2 * (i // 3)))
    out_i = load(0, IMG, img_h)

    def compact_grads(k):
        def body(t):
            at = rows_at(32 * k + T * t)
            for q in range(4):
                i = IDX[q, at]
                low, i = i < 128, i & 127
                for f, src in enumerate((CA, CB)):
                    halves = []
                    for x in (2 * q, 2 * q + 1):
                        v = src[x, at]
                        halves.append(jnp.where(low, take(v[:, :128], i), take(v[:, 128:], i)))
                    CG[k, f, q, t] = jnp.where(lane1 < 64, halves[0], halves[1])

        loop(4, body)

    g_c = []
    for i in (1 - zl, zl):
        compact_grads(2 * i + (1 - c))
        cp = rcopy(CG.at[2 * i + (1 - c)], RA.at[i], gs.at[i], gr.at[i], core)
        cp.start()
        g_c.append(cp)
    pair = 2 * (1 - zl) + c
    compact_grads(pair)
    g_c[0].wait()
    for f in range(2):
        for q in range(4):
            CG[pair, f, q] = CG[pair, f, q] + RA[1 - zl, f, q]
    g_z = rcopy(CG.at[pair], RBUF, gs.at[2], gr.at[2], zlo)
    g_z.start()
    g_c[1].wait()
    g_z.wait()

    def spread(t):
        at, to = rows_at(32 * s + T * t), rows_at(T * t)
        for q in range(4):
            for f, src, out in ((0, CA, GA), (1, CB, GB)):
                v = RA[zl, f, q, t] + RBUF[f, q, t]
                for x in (2 * q, 2 * q + 1):
                    i = INV[x, t]
                    have, i = i >= 0, i & 127
                    g = jnp.concatenate([take(v, i[:, :128]), take(v, i[:, 128:])], axis=1)
                    out[x, to] = src[x, at] + jnp.where(have, g, 0.0)

    loop(4, spread)
    out_g = load(1, GA, gg_h)
    out_b = load(2, GB, bg_h)
    out_i.wait()
    out_g.wait()
    out_b.wait()


def shards(
    state_before, state_now, base_model, buoyancy, latent, flow_gain, flow_bias, records, source_wavelet, source_cell,
    shot, receiver_depth,
):
    any_ = pl.BlockSpec(memory_space=pl.ANY)
    smem = pl.BlockSpec(memory_space=pltpu.SMEM)
    vmem = pl.BlockSpec(memory_space=pltpu.VMEM)
    field = (8, 128, 256)
    halo = (14, 144, 256)
    pick, shift = tables()
    img, gg, bg = pl.pallas_call(
        kernel,
        out_shape=(
            jax.ShapeDtypeStruct(field, F32),
            jax.ShapeDtypeStruct((8, 32, 256), F32),
            jax.ShapeDtypeStruct((8, 32, 256), F32),
        ),
        in_specs=[any_] * 8 + [smem] * 3 + [vmem] * 3,
        out_specs=(any_, any_, any_),
        scratch_shapes=[
            pltpu.VMEM((4,) + halo, F32),
            pltpu.VMEM(halo, F32),
            pltpu.VMEM(field, F32),
            pltpu.VMEM(field, F32),
            pltpu.VMEM(field, F32),
            pltpu.VMEM((4, 2, 8, 32, 256), jnp.bfloat16),
            pltpu.VMEM((2, 256, 128), jnp.bfloat16),
            pltpu.VMEM((4, 14, 128, 256), F32),
            pltpu.VMEM((5, 14, 128, 256), F32),
            pltpu.VMEM((14, 128, 256), F32),
            pltpu.VMEM(field, F32),
            pltpu.VMEM((13, 128, 256), F32),
            pltpu.VMEM((12, 136, 256), F32),
            pltpu.VMEM((12, 128, 256), F32),
            pltpu.VMEM((12, 128, 256), F32),
            pltpu.VMEM((14, 128, 128), F32),
            pltpu.VMEM((4, 14, 128, 128), F32),
            pltpu.VMEM((128, 256), F32),
            pltpu.VMEM(field, F32),
            pltpu.VMEM(field, F32),
            pltpu.VMEM(field, F32),
            pltpu.VMEM((8, 32, 256), F32),
            pltpu.VMEM((8, 32, 256), F32),
            pltpu.VMEM((4, 2, 4, 4, 8, 128), F32),
            pltpu.VMEM((2, 2, 4, 4, 8, 128), F32),
            pltpu.VMEM((2, 4, 4, 8, 128), F32),
            pltpu.VMEM((7, 64, 128), F32),
            pltpu.VMEM((7, 16, 128), F32),
            pltpu.VMEM((3, 8, 128), F32),
            pltpu.VMEM((4, 8, 128), F32),
            pltpu.VMEM((8, 128), F32),
            pltpu.VMEM((2, 8, 128), F32),
            pltpu.VMEM((4, 128, 128), I32),
            pltpu.VMEM((8, 4, 8, 256), I32),
            pltpu.VMEM((128, 128), I32),
            pltpu.VMEM((128, 128), I32),
            pltpu.VMEM((6, 16, 8, 256), I32),
            pltpu.VMEM((2, 2, 128, 256), jnp.int16),
            pltpu.VMEM((2, 2, 128, 256), jnp.int16),
            pltpu.VMEM((3, 2, 8, 8, 128), F32),
            pltpu.VMEM((3, 2, 8, 8, 128), F32),
            pltpu.VMEM((128, 128), F32),
            pltpu.VMEM((2, 8, 128), F32),
            pltpu.VMEM((2, 8, 128), F32),
            pltpu.SemaphoreType.DMA((8,)),
            pltpu.SemaphoreType.DMA((2,)),
            pltpu.SemaphoreType.DMA((2,)),
            pltpu.SemaphoreType.DMA((3, 2)),
            pltpu.SemaphoreType.DMA((3, 2)),
            pltpu.SemaphoreType.DMA((3,)),
            pltpu.SemaphoreType.DMA((3,)),
            pltpu.SemaphoreType.DMA((3,)),
            pltpu.SemaphoreType.DMA((3,)),
            pltpu.SemaphoreType.DMA((10,)),
            pltpu.SemaphoreType.DMA((10,)),
            pltpu.SemaphoreType.DMA((4,)),
            pltpu.SemaphoreType.DMA((4,)),
        ],
        compiler_params=pltpu.CompilerParams(
            collective_id=1, has_side_effects=True, vmem_limit_bytes=58 << 20
        ),
        name="flow_gradient",
    )(
        state_before[0], state_now[0], base_model, buoyancy, latent[0], flow_gain, flow_bias, records, source_wavelet,
        source_cell, shot, receiver_depth, jnp.asarray(pick, jnp.bfloat16), jnp.asarray(shift),
    )
    return img[None], gg, bg


def solution(mesh):
    in_specs = (
        P("smp", "dom", None, None),
        P("smp", "dom", None, None),
        P("dom", None, None),
        P("dom", None, None),
        P("smp", "dom", None, None),
        P("dom", "smp", None),
        P("dom", "smp", None),
        P("dom", None, None, None),
        P(),
        P(),
        P(),
        P("dom", None),
    )
    out_specs = (P("smp", "dom", None, None), P("dom", "smp", None), P("dom", "smp", None))
    return jax.shard_map(shards, mesh=mesh, in_specs=in_specs, out_specs=out_specs, check_vma=False)
```

```python
import functools

import jax
import jax.numpy as jnp
import numpy as np
from jax import lax
from jax.experimental import pallas as pl
from jax.experimental.pallas import tpu as pltpu
from jax.sharding import PartitionSpec as P

MESH = pl.DeviceIdType.MESH
I32 = jnp.int32


def ball(radius):
    return [(a, b) for a in range(-radius, radius + 1) for b in range(abs(a) - radius, radius - abs(a) + 1)]


def near(plane):
    return [(plane + a, y, z) for a in range(-3, 4) for y, z in ball(3 - abs(a))]


def across(height):
    radius = {1: {0: 2, -1: 2, 1: 1, -2: 1, 2: 0, -3: 0}, 2: {0: 1, -1: 1, -2: 1, 1: 0, -3: 0}, 3: {0: 0, -2: 0, -3: 0}}
    return [(p, y, z) for p, r in radius[height].items() for y, z in ball(r)]


COUNTS = [len(across(h)) for h in (1, 2, 3)]
STARTS = [sum(COUNTS[:h]) for h in range(4)]


SPARE = 58
USCALE = 32767.0 / 6.0
BSCALE = 65532.0


def bands(cells, base=0):
    out = {}
    for i, (p, y, z) in enumerate(cells):
        w, first = out.get((p, y), (0, base + i))
        out[p, y] = (max(w, abs(z)), first)
    return out


def tables():
    up = sum((across(h) for h in (1, 2, 3)), [])
    down = [(-1 - p, y, z) for p, y, z in up]
    right = [[(p + 8, y, z) for p, y, z in cells] for cells in (up, down)]
    lists = [near(x) for x in range(8)] + [down, right[0]]
    pick = np.zeros((128, 64 * len(lists)), np.float32)
    shift = np.zeros((8, 64 * len(lists)), np.float32)
    for i, cells in enumerate(lists):
        if i >= 8:
            cells = cells + [{8: (-1, 0, 0), 9: (8, 0, 0)}[i]]
        cells = cells + [cells[0]] * (64 - len(cells))
        for j, (p, y, z) in enumerate(cells):
            pick[16 * (y + 3) + p + 3, 64 * i + j] = 1.0
            shift[:, 64 * i + j] = z
    return pick, shift


F32 = jnp.float32
PAD = 8
T = 8
G = 128


def kernel(
    sb_h, sn_h, base_h, buoy_h, lat_h, gain_h, bias_h, rec_h, wav, cell, shot, depth, pick, shift,
    img_h, gg_h, bg_h,
    U, B, SB, BASE, LAT, PG, RQ, LU, AA, M, Q, CX, CYP, CYM, CZP, CZM, DG, DB, RB, KEY, HIT, IMG, CA, CB, GA, GB, CG, RA, RBUF,
    RX, RY, RZ, RALL, DS, DH, IDX, INV, SIDX, INVH, SE, RE, SG, RG, KT, SR, RR,
    lsem, es, er, hs, hr, ps, pr, gs, gr, rs, rr, ds_, dr_,
):
    d = lax.axis_index("dom")
    s = lax.axis_index("smp")
    gx, gy, gz = d // 8, (d // 2) % 4, d % 2
    zl, c = s // 2, s % 2
    left, right = ((d + 31) % 32, s), ((d + 1) % 32, s)
    core = (d, 2 * zl + (1 - c))
    zlo = (d, 2 * (1 - zl) + c)
    far = (d, 2 * (1 - zl) + (1 - c))
    xs = [(((gx + k) % 4) * 8 + d % 8, s) for k in (1, 2, 3)]
    ys = [(gx * 8 + ((gy + k) % 4) * 2 + gz, s) for k in (1, 2, 3)]
    zs = (d - gz + (1 - gz), s)

    def load(i, src, dst):
        cp = pltpu.make_async_copy(src, dst, lsem.at[i])
        cp.start()
        return cp

    rows = pl.ds(PAD, 128)
    own = pl.ds(3, 8)
    ld_g = load(2, gain_h, PG.at[s, 0])
    ld_c = load(3, bias_h, PG.at[s, 1])
    ld_u = load(0, sn_h, U.at[0, own, rows])
    ld_b = load(1, buoy_h, B.at[own, rows])
    ld_r = load(4, rec_h.at[:, s], RQ)
    ld_base = load(5, base_h, BASE)
    ld_lat = load(6, lat_h, LAT)
    ld_sb = load(7, sb_h, SB)

    barrier = pltpu.get_barrier_semaphore()
    peers = [left, right, core, zlo, far] + xs + ys
    for p in peers:
        pl.semaphore_signal(barrier, inc=1, device_id=p, device_id_type=MESH)

    def rcopy(src, dst, ss, sr, dev):
        return pltpu.make_async_remote_copy(
            src_ref=src, dst_ref=dst, send_sem=ss, recv_sem=sr, device_id=dev, device_id_type=MESH
        )

    def loop(n, body, per=1):
        def run(i, _):
            for k in range(per):
                body(i * per + k if per > 1 else i)
            return 0

        lax.fori_loop(0, n // per, run, 0)

    def rows_at(first, n=T):
        if isinstance(first, int):
            return slice(first, first + n)
        return pl.ds(pl.multiple_of(first, T), n)

    def planes(n, body):
        loop(n, lambda i: body(i, 0))

    zero = jnp.zeros((T, 256), F32)
    lane = lax.broadcasted_iota(I32, (T, 256), 1)
    lane1 = lax.broadcasted_iota(I32, (T, 128), 1)
    lane_f = lane.astype(F32)
    sub = lax.broadcasted_iota(I32, (T, 256), 0)

    def tile(j):
        return slice(T * j, T * j + T)

    def padded(j):
        return slice(PAD + T * j, PAD + T * j + T)

    def twice(v):
        return jnp.concatenate([v, v], axis=1)

    def clear(i):
        for n in range(4):
            U[n, i, 0:8] = zero
            U[n, i, 136:144] = zero
        B[i, 0:8] = zero
        B[i, 136:144] = zero
        for j in range(16):
            AA[4, i, tile(j)] = zero

    loop(14, clear)

    picked = shot[0]
    flat = cell[picked]
    cell_x = flat // (128 * 256)
    cell_y = (flat // 256) % 128
    cell_z = flat % 256
    for j in range(16):
        HIT[tile(j)] = jnp.where((sub + T * j == cell_y) & (lane == cell_z), 1.0, 0.0)
    DS[...] = depth[...].astype(F32)

    ld_u.wait()
    ld_b.wait()
    for e, p in enumerate((0, 7)):
        for j in range(8):
            sl = slice(16 * j, 16 * j + 16)
            at = slice(PAD + 16 * j, PAD + 16 * j + 16)
            SE[e, 0, sl] = jnp.round(U[0, p + 3, at] * USCALE).astype(I32).astype(jnp.int16)
            SE[e, 1, sl] = jnp.round((B[p + 3, at] - 1.0) * BSCALE).astype(I32).astype(jnp.int16)

    ld_g.wait()
    ld_c.wait()
    pl.semaphore_wait(barrier, len(peers))

    d_l = rcopy(DS, DH.at[1], ds_.at[0], dr_.at[0], left)
    d_r = rcopy(DS, DH.at[0], ds_.at[1], dr_.at[1], right)
    d_l.start()
    d_r.start()
    p_z = rcopy(PG.at[s], PG.at[s], ps.at[0], pr.at[0], zlo)
    p_c = rcopy(PG.at[s], PG.at[s], ps.at[1], pr.at[1], core)
    e_l = rcopy(SE.at[0], RE.at[1], es.at[0], er.at[0], left)
    e_r = rcopy(SE.at[1], RE.at[0], es.at[1], er.at[1], right)
    e_l.start()
    e_r.start()
    p_z.start()
    p_c.start()

    ld_r.wait()
    mine = (picked // 2 == d).astype(F32)
    odd = (picked % 2).astype(F32)
    for k in range(4):
        r0 = RQ[0, 64 * k : 64 * k + 64].astype(F32)
        r1 = RQ[1, 64 * k : 64 * k + 64].astype(F32)
        RX[k] = (r0 * (1.0 - odd) + r1 * odd) * mine
    r_x = []
    for k in (1, 2, 3):
        cp = rcopy(RX.at[(gx + k) % 4], RX.at[3 + k], rs.at[k - 1], rr.at[k - 1], xs[k - 1])
        cp.start()
        r_x.append(cp)

    def shifted(ref, at, y):
        t = [ref[at + (rows_at(PAD + y - T),)], ref[at + (rows_at(PAD + y),)]]
        for i in range(1, G // T + 1):
            t.append(ref[at + (rows_at(PAD + y + T * i),)])
            after = pltpu.roll(jnp.where(sub == 0, t[i + 1], t[i]), T - 1, 0)
            before = pltpu.roll(jnp.where(sub == T - 1, t[i - 1], t[i]), 1, 0)
            yield t[i], after, before

    def coef(p, y):
        for i, (b, after, before) in enumerate(shifted(B, (p + 3,), y)):
            sl, at = rows_at(y + T * i), rows_at(PAD + y + T * i)
            xp, xm = B[p + 4, at], B[p + 2, at]
            zn = jnp.where(lane == 255, 0.0, pltpu.roll(b, 255, 1))
            zp = jnp.where(lane == 0, 0.0, pltpu.roll(b, 1, 1))
            CX[p + 3, sl] = 0.5 * (b + xp)
            CX[p + 2, sl] = 0.5 * (b + xm)
            CYP[p + 2, sl] = 0.5 * (b + after)
            CYM[p + 2, sl] = 0.5 * (b + before)
            CZP[p + 2, sl] = jnp.where(lane == 255, 0.0, 0.5 * (b + zn))
            CZM[p + 2, sl] = jnp.where(lane == 0, 0.0, 0.5 * (b + zp))
            DG[p + 2, sl] = 3.0 * b + 0.5 * ((xp + xm) + (after + before) + (zn + zp))

    planes(6, lambda i, y: coef(i + 1, y))

    def laps(k, p, y):
        for i, (v, after, before) in enumerate(shifted(U, (k, p + 3), y)):
            sl, at = rows_at(y + T * i), rows_at(PAD + y + T * i)
            t = CX[p + 3, sl] * U[k, p + 4, at] + CX[p + 2, sl] * U[k, p + 2, at]
            t = t + (CYP[p + 2, sl] * after + CYM[p + 2, sl] * before)
            t = t + (CZP[p + 2, sl] * pltpu.roll(v, 255, 1) + CZM[p + 2, sl] * pltpu.roll(v, 1, 1))
            yield sl, at, v, t - DG[p + 2, sl] * v

    def first_lap(p, y):
        for sl, _, _, t in laps(0, p, y):
            LU[0, p + 3, sl] = t

    planes(6, lambda i, y: first_lap(i + 1, y))

    d_l.wait()
    d_r.wait()
    near_d = jnp.concatenate([DH[0, 5:8], DS[...], DH[1, 0:3], jnp.zeros((2, 128), F32)], axis=0)
    rolled = [near_d if y == 0 else pltpu.roll(near_d, (-y) % 128, 1) for y in range(-3, 4)]
    key = jnp.transpose(jnp.concatenate(rolled + [jnp.zeros((16, 128), F32)], axis=0))
    for p in range(14):
        DB[p] = jnp.broadcast_to(key[:, 48 + p : 49 + p], (128, 128))
    KEY[...] = key
    idx = jnp.dot(key.astype(jnp.bfloat16), pick[...], preferred_element_type=F32) + shift[0:1, :]
    idx = jnp.clip(idx, 0.0, 255.0).astype(I32)
    for q in range(4):
        IDX[q] = idx[:, 128 * q : 128 * q + 128]
    SIDX[...] = idx[:, 512:640]

    def take(v, i):
        return jnp.take_along_axis(v, i, axis=1, mode="promise_in_bounds")

    def compact(which, read, heights, spare=None):
        def body(t):
            halves = []
            for half in range(2):
                i = SIDX[pl.ds(pl.multiple_of(64 * half + T * t, T), T)]
                low, i = i < 128, i & 127
                for side in range(2):
                    for h in heights:
                        v = read(7 - h if side else h, 64 * half + T * t)
                        g = jnp.where(low, take(v[:, :128], i), take(v[:, 128:], i))
                        start = 64 * side + STARTS[h]
                        out = g if side == 0 and h == heights[0] else jnp.where(lane1 >= start, g, out)
                    if spare is not None:
                        v = spare(6 if side else 1, 64 * half + T * t)
                        g = jnp.where(low, take(v[:, :128], i), take(v[:, 128:], i))
                        out = jnp.where(lane1 == 64 * side + SPARE, g, out)
                halves.append(out)
            a, b = halves
            SG[which, 0, t] = jnp.where(lane1 < 64, a, pltpu.roll(b, 64, 1))
            SG[which, 1, t] = jnp.where(lane1 < 64, pltpu.roll(a, 64, 1), b)

        loop(8, body, 4)
        a = rcopy(SG.at[which, 0], RG.at[which, 1], hs.at[which, 0], hr.at[which, 0], left)
        b = rcopy(SG.at[which, 1], RG.at[which, 0], hs.at[which, 1], hr.at[which, 1], right)
        a.start()
        b.start()
        return a, b

    def at_ends(do):
        @pl.when(d == 0)
        def _():
            do(0)

        @pl.when(d == 31)
        def _():
            do(1)

    def expand(which, cps, write, heights):
        for cp in cps:
            cp.wait()

        def blank(side):
            for t in range(8):
                RG[which, side, t] = jnp.zeros((T, 128), F32)

        at_ends(blank)

        def body(t):
            for side in range(2):
                v = RG[which, side, t % 8]
                for h in heights:
                    i = INVH[3 * side + h, t]
                    g = jnp.concatenate([take(v, i[:, :128]), take(v, i[:, 128:])], axis=1)
                    write(8 + h if side else -1 - h, T * t, g)

        loop(16, body, 4)

    h_b = compact(
        0, lambda p, y: B[p + 3, rows_at(PAD + y)], (1, 2), lambda p, y: U[0, p + 3, rows_at(PAD + y)]
    )

    ups = [bands(across(h + 1), STARTS[h]) for h in range(3)]
    downs = [{(7 - p, y): v for (p, y), v in band.items()} for band in ups]

    def mark(invs, maps, cells):
        for p, y in sorted(set().union(*maps)):
            col = 16 * (y + 3) + p + 3
            off = lane_f - cells[:, col : col + 1]
            dist = jnp.abs(off)
            for i, band in enumerate(maps):
                if (p, y) in band:
                    w, base = band[p, y]
                    invs[i] = jnp.where(dist <= w, off + (base + w), invs[i])
        return invs

    def invert_halo(t):
        cells = KEY[rows_at(T * t)]
        for side, maps in enumerate((ups, downs)):
            invs = mark([jnp.zeros((T, 256), F32)] * 3, maps, cells)
            for h in range(3):
                INVH[3 * side + h, t] = invs[h].astype(I32) + 64 * (t // 8)

    loop(16, invert_halo, 2)

    def invert(t):
        cells = KEY[rows_at(32 * s + T * t)]
        maps = [bands(near(x), 64 * (x % 2)) for x in range(8)]
        invs = mark([jnp.full((T, 256), -1.0, F32)] * 8, maps, cells)
        for x in range(8):
            INV[x, t] = invs[x].astype(I32)

    loop(4, invert)

    p_z.wait_recv()
    other = 2 * (1 - zl) + c
    p_f = rcopy(PG.at[other], PG.at[other], ps.at[2], pr.at[2], core)
    p_f.start()

    for cp in r_x:
        cp.wait()
    for k in range(4):
        sl = pl.ds(16 * k, 16)
        RY[k] = RX[gx, sl] + RX[4, sl] + RX[5, sl] + RX[6, sl]
    r_y = []
    for k in (1, 2, 3):
        cp = rcopy(RY.at[(gy + k) % 4], RY.at[3 + k], rs.at[2 + k], rr.at[2 + k], ys[k - 1])
        cp.start()
        r_y.append(cp)

    e_l.wait()
    e_r.wait()
    for e, p in enumerate((-1, 8)):
        for j in range(8):
            sl = slice(16 * j, 16 * j + 16)
            at = slice(PAD + 16 * j, PAD + 16 * j + 16)
            U[0, p + 3, at] = RE[e, 0, sl].astype(I32).astype(F32) * (1.0 / USCALE)
            B[p + 3, at] = RE[e, 1, sl].astype(I32).astype(F32) * (1.0 / BSCALE) + 1.0

    def no_edge(side):
        for j in range(16):
            U[0, 11 if side else 2, padded(j)] = zero
            B[11 if side else 2, padded(j)] = zero

    at_ends(no_edge)
    planes(2, lambda i, y: coef(7 * i, y))
    planes(2, lambda i, y: first_lap(7 * i, y))
    ld_base.wait()
    ld_lat.wait()
    ld_sb.wait()
    p_c.wait()
    p_f.wait()
    p_z.wait_send()

    first = d * 8

    def pulse(n, p):
        return jnp.where(first + p == cell_x, wav[n, picked], 0.0)

    def step_one(p, y):
        factor = pulse(0, p)
        for i in range(G // 16):
            sl, at = rows_at(y + 16 * i, 16), rows_at(PAD + y + 16 * i, 16)
            k, o = i // 2, slice(16 * (i % 2), 16 * (i % 2) + 16)
            g = PG[k, 0, p, o].astype(F32)
            b = PG[k, 1, p, o].astype(F32)
            sq = jnp.tanh(LAT[p, sl] * g + b)
            m = BASE[p, sl] * jnp.exp(0.25 * sq)
            M[p + 3, sl] = m
            Q[p, sl] = m * 0.25 * (1.0 - sq * sq)
            new = 2.0 * U[0, p + 3, at] - SB[p, sl] + m * LU[0, p + 3, sl]
            U[1, p + 3, at] = new + factor * HIT[sl]

    planes(6, lambda i, y: step_one(i + 2 * (i // 3), y))
    h_u = compact(1, lambda p, y: U[1, p + 3, rows_at(PAD + y)], (0, 1, 2))
    h_m = compact(2, lambda p, y: M[p + 3, rows_at(y)], (0, 1, 2))
    planes(2, lambda i, y: step_one(i + 3, y))

    for cp in r_y:
        cp.wait()
    for k in range(2):
        sl = pl.ds(8 * k, 8)
        RZ[k] = RY[gy, sl] + RY[4, sl] + RY[5, sl] + RY[6, sl]
    r_z = rcopy(RZ.at[1 - gz], RZ.at[2], rs.at[6], rr.at[6], zs)
    r_z.start()

    def write_b(p, y, g):
        B[p + 3, rows_at(PAD + y)] = g

    expand(0, h_b, write_b, (1, 2))

    def second(t):
        slot = jnp.full((T, 128), SPARE, I32) + 64 * (t // 8)
        for side in range(2):
            U[0, 12 if side else 1, rows_at(PAD + T * t)] = twice(take(RG[0, side, t % 8], slot))

    loop(16, second, 4)
    planes(4, lambda i, y: coef(i - 2 + 8 * (i // 2), y))

    r_z.wait()
    RALL[s] = RZ[gz] + RZ[2]
    r_s = []
    for i, p in enumerate((core, zlo, far)):
        cp = rcopy(RALL.at[s], RALL.at[s], rs.at[7 + i], rr.at[7 + i], p)
        cp.start()
        r_s.append(cp)

    def advance(n, p):
        factor = pulse(n, p)
        for sl, at, v, a in laps(n, p, 0):
            m = M[p + 3, sl]
            LU[n, p + 3, sl] = a
            new = 2.0 * v - U[n - 1, p + 3, at] + m * a + factor * HIT[sl]
            r = jnp.where(lane_f == twice(DB[p + 3, sl]), new - twice(RB[n, p + 3, sl]), 0.0)
            AA[n, p + 3, sl] = r
            yield sl, at, m, new, r

    def step(n, p, y):
        for _, at, _, new, _ in advance(n, p):
            U[n + 1, p + 3, at] = new

    def last_step(p, y):
        for _, at, m, _, r in advance(3, p):
            U[0, p + 3, at] = m * r

    for cp in r_s:
        cp.wait()
    rt = jnp.transpose(jnp.concatenate([RALL[k] for k in range(4)] + [jnp.zeros((96, 128), F32)], axis=0))
    for k in range(4):
        for x in range(8):
            RB[k, x + 3] = jnp.broadcast_to(rt[:, 8 * k + x : 8 * k + x + 1], (128, 128))

    def inside(t, _):
        planes(6 - 2 * t, lambda i, y: step(1 + t, 1 + t + i, y))
        return 0

    lax.fori_loop(0, 2, inside, 0)
    planes(2, lambda i, y: last_step(3 + i, y))

    def write_u(p, y, g):
        U[1, p + 3, rows_at(PAD + y)] = g

    def write_m(p, y, g):
        M[p + 3, rows_at(y)] = g

    expand(1, h_u, write_u, (0, 1, 2))

    expand(2, h_m, write_m, (0, 1, 2))

    def outside(t, _):
        planes(6, lambda i, y: step(1 + t, t - 2 + i + (6 - 2 * t) * (i // 3), y))
        return 0

    lax.fori_loop(0, 2, outside, 0)
    planes(6, lambda i, y: last_step(i + 2 * (i // 3), y))

    sends = [(3, 0), (3, 1), (3, 2), (2, 0), (2, 1), (1, 0)]

    def pack(t):
        at = rows_at(T * t)
        out = jnp.zeros((T, 128), F32)
        for side in range(2):
            for i, (k, h) in enumerate(sends):
                total = jnp.sum(AA[k, 3 + (7 - h if side else h), at], axis=1, keepdims=True)
                out = jnp.where(lane1 == 8 * side + i, total, out)
        KT[at] = out

    loop(16, pack, 4)
    packed = jnp.transpose(KT[...])
    SR[0] = packed[0:8]
    SR[1] = packed[8:16]
    r_l = rcopy(SR.at[0], RR.at[1], ds_.at[2], dr_.at[2], left)
    r_r = rcopy(SR.at[1], RR.at[0], ds_.at[3], dr_.at[3], right)
    r_l.start()
    r_r.start()

    def back(k, p, y):
        for sl, at, _, t in laps(3 - k, p, y):
            a = AA[k - 1, p + 3, sl] + t + 2.0 * AA[k, p + 3, sl] - AA[k + 1, p + 3, sl]
            AA[k - 1, p + 3, sl] = a
            U[4 - k, p + 3, at] = M[p + 3, sl] * a

    def finish(p, y):
        for sl, at, _, t in laps(2, p, y):
            a2, a3 = AA[1, p + 3, sl], AA[2, p + 3, sl]
            a1 = AA[0, p + 3, sl] + t + 2.0 * a2 - a3
            img = AA[3, p + 3, sl] * LU[3, p + 3, sl] + a3 * LU[2, p + 3, sl]
            img = img + a2 * LU[1, p + 3, sl] + a1 * LU[0, p + 3, sl]
            IMG[p, sl] = img
            com = img * Q[p, sl]
            CB[p, sl] = com
            CA[p, sl] = com * LAT[p, sl]

    def resid_one(p, y):
        for i in range(G // T):
            sl = rows_at(y + T * i)
            r = U[1, p + 3, rows_at(PAD + y + T * i)] - twice(RB[0, p + 3, sl])
            AA[0, p + 3, sl] = jnp.where(lane_f == twice(DB[p + 3, sl]), r, 0.0)

    planes(8, resid_one)

    def inside_back(t, _):
        planes(6 - 2 * t, lambda i, y: back(3 - t, 1 + t + i, y))
        return 0

    lax.fori_loop(0, 2, inside_back, 0)
    planes(2, lambda i, y: finish(3 + i, y))

    r_l.wait()
    r_r.wait()

    def no_resid(side):
        RR[side] = jnp.zeros((8, 128), F32)

    at_ends(no_resid)
    KT[...] = jnp.transpose(jnp.concatenate([RR[0], RR[1], jnp.zeros((112, 128), F32)], axis=0))
    for side in range(2):
        for i, (k, h) in enumerate(sends):
            p = 8 + h if side else -1 - h
            for j in range(16):
                sl = tile(j)
                col = 8 * side + i
                r = jnp.where(lane_f == twice(DB[p + 3, sl]), KT[sl, col : col + 1], 0.0)
                AA[k, p + 3, sl] = r
                if k == 3:
                    U[0, p + 3, padded(j)] = M[p + 3, sl] * r

    def outside_back(t, _):
        planes(6, lambda i, y: back(3 - t, t - 2 + i + (6 - 2 * t) * (i // 3), y))
        return 0

    lax.fori_loop(0, 2, outside_back, 0)
    planes(6, lambda i, y: finish(i + 2 * (i // 3), y))
    out_i = load(0, IMG, img_h)

    def compact_grads(k):
        def body(t):
            at = rows_at(32 * k + T * t)
            for q in range(4):
                i = IDX[q, at]
                low, i = i < 128, i & 127
                for f, src in enumerate((CA, CB)):
                    halves = []
                    for x in (2 * q, 2 * q + 1):
                        v = src[x, at]
                        halves.append(jnp.where(low, take(v[:, :128], i), take(v[:, 128:], i)))
                    CG[k, f, q, t] = jnp.where(lane1 < 64, halves[0], halves[1])

        loop(4, body)

    g_c = []
    for i in (1 - zl, zl):
        compact_grads(2 * i + (1 - c))
        cp = rcopy(CG.at[2 * i + (1 - c)], RA.at[i], gs.at[i], gr.at[i], core)
        cp.start()
        g_c.append(cp)
    pair = 2 * (1 - zl) + c
    compact_grads(pair)
    g_c[0].wait()
    for f in range(2):
        for q in range(4):
            CG[pair, f, q] = CG[pair, f, q] + RA[1 - zl, f, q]
    g_z = rcopy(CG.at[pair], RBUF, gs.at[2], gr.at[2], zlo)
    g_z.start()
    g_c[1].wait()
    g_z.wait()

    def spread(t):
        at, to = rows_at(32 * s + T * t), rows_at(T * t)
        for q in range(4):
            for f, src, out in ((0, CA, GA), (1, CB, GB)):
                v = RA[zl, f, q, t] + RBUF[f, q, t]
                for x in (2 * q, 2 * q + 1):
                    i = INV[x, t]
                    have, i = i >= 0, i & 127
                    g = jnp.concatenate([take(v, i[:, :128]), take(v, i[:, 128:])], axis=1)
                    out[x, to] = src[x, at] + jnp.where(have, g, 0.0)

    loop(4, spread)
    out_g = load(1, GA, gg_h)
    out_b = load(2, GB, bg_h)
    out_i.wait()
    out_g.wait()
    out_b.wait()


def hand_out(img, gg, bg, img_o, gg_o, bg_o, vi, vg, vb, sem):
    moves = [(img.at[p], vi.at[p], img_o.at[p]) for p in range(8)] + [(gg, vg, gg_o), (bg, vb, bg_o)]
    come = [pltpu.make_async_copy(a, b, sem.at[0, i]) for i, (a, b, _) in enumerate(moves)]
    go = [pltpu.make_async_copy(b, o, sem.at[1, i]) for i, (_, b, o) in enumerate(moves)]
    for cp in come:
        cp.start()
    for a, b in zip(come, go):
        a.wait()
        b.start()
    for cp in go:
        cp.wait()


def shards(
    state_before, state_now, base_model, buoyancy, latent, flow_gain, flow_bias, records, source_wavelet, source_cell,
    shot, receiver_depth,
):
    any_ = pl.BlockSpec(memory_space=pl.ANY)
    smem = pl.BlockSpec(memory_space=pltpu.SMEM)
    vmem = pl.BlockSpec(memory_space=pltpu.VMEM)
    field = (8, 128, 256)
    halo = (14, 144, 256)
    pick, shift = tables()
    results = (
        jax.ShapeDtypeStruct(field, F32),
        jax.ShapeDtypeStruct((8, 32, 256), F32),
        jax.ShapeDtypeStruct((8, 32, 256), F32),
    )
    made = pl.pallas_call(
        kernel,
        out_shape=results,
        in_specs=[any_] * 8 + [smem] * 3 + [vmem] * 3,
        out_specs=(any_, any_, any_),
        scratch_shapes=[
            pltpu.VMEM((4,) + halo, F32),
            pltpu.VMEM(halo, F32),
            pltpu.VMEM(field, F32),
            pltpu.VMEM(field, F32),
            pltpu.VMEM(field, F32),
            pltpu.VMEM((4, 2, 8, 32, 256), jnp.bfloat16),
            pltpu.VMEM((2, 256, 128), jnp.bfloat16),
            pltpu.VMEM((4, 14, 128, 256), F32),
            pltpu.VMEM((5, 14, 128, 256), F32),
            pltpu.VMEM((14, 128, 256), F32),
            pltpu.VMEM(field, F32),
            pltpu.VMEM((13, 128, 256), F32),
            pltpu.VMEM((12, 128, 256), F32),
            pltpu.VMEM((12, 128, 256), F32),
            pltpu.VMEM((12, 128, 256), F32),
            pltpu.VMEM((12, 128, 256), F32),
            pltpu.VMEM((12, 128, 256), F32),
            pltpu.VMEM((14, 128, 128), F32),
            pltpu.VMEM((4, 14, 128, 128), F32),
            pltpu.VMEM((128, 128), F32),
            pltpu.VMEM((128, 256), F32),
            pltpu.VMEM(field, F32),
            pltpu.VMEM(field, F32),
            pltpu.VMEM(field, F32),
            pltpu.VMEM((8, 32, 256), F32),
            pltpu.VMEM((8, 32, 256), F32),
            pltpu.VMEM((4, 2, 4, 4, 8, 128), F32),
            pltpu.VMEM((2, 2, 4, 4, 8, 128), F32),
            pltpu.VMEM((2, 4, 4, 8, 128), F32),
            pltpu.VMEM((7, 64, 128), F32),
            pltpu.VMEM((7, 16, 128), F32),
            pltpu.VMEM((3, 8, 128), F32),
            pltpu.VMEM((4, 8, 128), F32),
            pltpu.VMEM((8, 128), F32),
            pltpu.VMEM((2, 8, 128), F32),
            pltpu.VMEM((4, 128, 128), I32),
            pltpu.VMEM((8, 4, 8, 256), I32),
            pltpu.VMEM((128, 128), I32),
            pltpu.VMEM((6, 16, 8, 256), I32),
            pltpu.VMEM((2, 2, 128, 256), jnp.int16),
            pltpu.VMEM((2, 2, 128, 256), jnp.int16),
            pltpu.VMEM((3, 2, 8, 8, 128), F32),
            pltpu.VMEM((3, 2, 8, 8, 128), F32),
            pltpu.VMEM((128, 128), F32),
            pltpu.VMEM((2, 8, 128), F32),
            pltpu.VMEM((2, 8, 128), F32),
            pltpu.SemaphoreType.DMA((8,)),
            pltpu.SemaphoreType.DMA((2,)),
            pltpu.SemaphoreType.DMA((2,)),
            pltpu.SemaphoreType.DMA((3, 2)),
            pltpu.SemaphoreType.DMA((3, 2)),
            pltpu.SemaphoreType.DMA((3,)),
            pltpu.SemaphoreType.DMA((3,)),
            pltpu.SemaphoreType.DMA((3,)),
            pltpu.SemaphoreType.DMA((3,)),
            pltpu.SemaphoreType.DMA((10,)),
            pltpu.SemaphoreType.DMA((10,)),
            pltpu.SemaphoreType.DMA((4,)),
            pltpu.SemaphoreType.DMA((4,)),
        ],
        compiler_params=pltpu.CompilerParams(
            collective_id=1, has_side_effects=True, vmem_limit_bytes=58 << 20
        ),
        name="flow_gradient",
    )(
        state_before[0], state_now[0], base_model, buoyancy, latent[0], flow_gain, flow_bias, records, source_wavelet.T,
        source_cell, shot, receiver_depth, jnp.asarray(pick, jnp.bfloat16), jnp.asarray(shift),
    )
    img, gg, bg = pl.pallas_call(
        hand_out,
        out_shape=results,
        in_specs=[any_] * 3,
        out_specs=(any_,) * 3,
        scratch_shapes=[pltpu.VMEM(r.shape, F32) for r in results] + [pltpu.SemaphoreType.DMA((2, 10))],
        name="hand_out",
    )(*made)
    return img[None], gg, bg


def solution(mesh):
    in_specs = (
        P("smp", "dom", None, None),
        P("smp", "dom", None, None),
        P("dom", None, None),
        P("dom", None, None),
        P("smp", "dom", None, None),
        P("dom", "smp", None),
        P("dom", "smp", None),
        P("dom", None, None, None),
        P(),
        P(),
        P(),
        P("dom", None),
    )
    out_specs = (P("smp", "dom", None, None), P("dom", "smp", None), P("dom", "smp", None))
    return jax.shard_map(shards, mesh=mesh, in_specs=in_specs, out_specs=out_specs, check_vma=False)
```

```python
import functools

import jax
import jax.numpy as jnp
import numpy as np
from jax import lax
from jax.experimental import pallas as pl
from jax.experimental.pallas import tpu as pltpu
from jax.sharding import PartitionSpec as P

MESH = pl.DeviceIdType.MESH
I32 = jnp.int32


def ball(radius):
    return [(a, b) for a in range(-radius, radius + 1) for b in range(abs(a) - radius, radius - abs(a) + 1)]


def near(plane):
    return [(plane + a, y, z) for a in range(-3, 4) for y, z in ball(3 - abs(a))]


def across(height):
    radius = {1: {0: 2, -1: 2, 1: 1, -2: 1, 2: 0, -3: 0}, 2: {0: 1, -1: 1, -2: 1, 1: 0, -3: 0}, 3: {0: 0, -2: 0, -3: 0}}
    return [(p, y, z) for p, r in radius[height].items() for y, z in ball(r)]


COUNTS = [len(across(h)) for h in (1, 2, 3)]
STARTS = [sum(COUNTS[:h]) for h in range(4)]


SPARE = 58
USCALE = 32767.0 / 6.0
BSCALE = 65532.0


def bands(cells, base=0):
    out = {}
    for i, (p, y, z) in enumerate(cells):
        w, first = out.get((p, y), (0, base + i))
        out[p, y] = (max(w, abs(z)), first)
    return out


def tables():
    up = sum((across(h) for h in (1, 2, 3)), [])
    down = [(-1 - p, y, z) for p, y, z in up]
    right = [[(p + 8, y, z) for p, y, z in cells] for cells in (up, down)]
    lists = [near(x) for x in range(8)] + [down, right[0]]
    pick = np.zeros((128, 64 * len(lists)), np.float32)
    shift = np.zeros((8, 64 * len(lists)), np.float32)
    for i, cells in enumerate(lists):
        if i >= 8:
            cells = cells + [{8: (-1, 0, 0), 9: (8, 0, 0)}[i]]
        cells = cells + [cells[0]] * (64 - len(cells))
        for j, (p, y, z) in enumerate(cells):
            pick[16 * (y + 3) + p + 3, 64 * i + j] = 1.0
            shift[:, 64 * i + j] = z
    return pick, shift


F32 = jnp.float32
PAD = 8
T = 8
G = 128


def kernel(
    sb_h, sn_h, base_h, buoy_h, lat_h, gain_h, bias_h, rec_h, wav, cell, shot, depth, pick, shift,
    img_h, gg_h, bg_h,
    U, B, SB, BASE, LAT, PG, RQ, LU, AA, M, Q, CX, CYP, CYM, CZP, CZM, DG, DB, RB, KEY, HIT, IMG, CA, CB, GA, GB, CG, RA, RBUF,
    RX, RY, RZ, RALL, DS, DH, IDX, INV, SIDX, INVH, SE, RE, SG, RG, KT, SR, RR,
    lsem, osem, es, er, hs, hr, ps, pr, gs, gr, rs, rr, ds_, dr_,
):
    d = lax.axis_index("dom")
    s = lax.axis_index("smp")
    gx, gy, gz = d // 8, (d // 2) % 4, d % 2
    zl, c = s // 2, s % 2
    left, right = ((d + 31) % 32, s), ((d + 1) % 32, s)
    core = (d, 2 * zl + (1 - c))
    zlo = (d, 2 * (1 - zl) + c)
    far = (d, 2 * (1 - zl) + (1 - c))
    xs = [(((gx + k) % 4) * 8 + d % 8, s) for k in (1, 2, 3)]
    ys = [(gx * 8 + ((gy + k) % 4) * 2 + gz, s) for k in (1, 2, 3)]
    zs = (d - gz + (1 - gz), s)

    def load(i, src, dst):
        cp = pltpu.make_async_copy(src, dst, lsem.at[i])
        cp.start()
        return cp

    rows = pl.ds(PAD, 128)
    own = pl.ds(3, 8)
    ld_g = load(2, gain_h, PG.at[s, 0])
    ld_c = load(3, bias_h, PG.at[s, 1])
    ld_u = load(0, sn_h, U.at[0, own, rows])
    ld_b = load(1, buoy_h, B.at[own, rows])
    ld_r = load(4, rec_h.at[:, s], RQ)
    ld_base = load(5, base_h, BASE)
    ld_lat = load(6, lat_h, LAT)
    ld_sb = load(7, sb_h, SB)

    barrier = pltpu.get_barrier_semaphore()
    peers = [left, right, core, zlo, far] + xs + ys
    for p in peers:
        pl.semaphore_signal(barrier, inc=1, device_id=p, device_id_type=MESH)

    def rcopy(src, dst, ss, sr, dev):
        return pltpu.make_async_remote_copy(
            src_ref=src, dst_ref=dst, send_sem=ss, recv_sem=sr, device_id=dev, device_id_type=MESH
        )

    def loop(n, body, per=1):
        def run(i, _):
            for k in range(per):
                body(i * per + k if per > 1 else i)
            return 0

        lax.fori_loop(0, n // per, run, 0)

    def rows_at(first, n=T):
        if isinstance(first, int):
            return slice(first, first + n)
        return pl.ds(pl.multiple_of(first, T), n)

    def planes(n, body):
        loop(n, lambda i: body(i, 0))

    zero = jnp.zeros((T, 256), F32)
    lane = lax.broadcasted_iota(I32, (T, 256), 1)
    lane1 = lax.broadcasted_iota(I32, (T, 128), 1)
    lane_f = lane.astype(F32)
    sub = lax.broadcasted_iota(I32, (T, 256), 0)

    def tile(j):
        return slice(T * j, T * j + T)

    def padded(j):
        return slice(PAD + T * j, PAD + T * j + T)

    def twice(v):
        return jnp.concatenate([v, v], axis=1)

    def clear(i):
        for n in range(4):
            U[n, i, 0:8] = zero
            U[n, i, 136:144] = zero
        B[i, 0:8] = zero
        B[i, 136:144] = zero
        for j in range(16):
            AA[4, i, tile(j)] = zero

    loop(14, clear)

    picked = shot[0]
    flat = cell[picked]
    cell_x = flat // (128 * 256)
    cell_y = (flat // 256) % 128
    cell_z = flat % 256
    for j in range(16):
        HIT[tile(j)] = jnp.where((sub + T * j == cell_y) & (lane == cell_z), 1.0, 0.0)
    DS[...] = depth[...].astype(F32)

    ld_u.wait()
    ld_b.wait()
    for e, p in enumerate((0, 7)):
        for j in range(8):
            sl = slice(16 * j, 16 * j + 16)
            at = slice(PAD + 16 * j, PAD + 16 * j + 16)
            SE[e, 0, sl] = jnp.round(U[0, p + 3, at] * USCALE).astype(I32).astype(jnp.int16)
            SE[e, 1, sl] = jnp.round((B[p + 3, at] - 1.0) * BSCALE).astype(I32).astype(jnp.int16)

    ld_g.wait()
    ld_c.wait()
    pl.semaphore_wait(barrier, len(peers))

    d_l = rcopy(DS, DH.at[1], ds_.at[0], dr_.at[0], left)
    d_r = rcopy(DS, DH.at[0], ds_.at[1], dr_.at[1], right)
    d_l.start()
    d_r.start()
    p_z = [rcopy(PG.at[s, f], PG.at[s, f], ps.at[0, f], pr.at[0, f], zlo) for f in range(2)]
    p_c = rcopy(PG.at[s], PG.at[s], ps.at[1, 0], pr.at[1, 0], core)
    p_z[0].start()
    p_z[1].start()
    e_l = rcopy(SE.at[0], RE.at[1], es.at[0], er.at[0], left)
    e_r = rcopy(SE.at[1], RE.at[0], es.at[1], er.at[1], right)
    e_l.start()
    e_r.start()
    p_c.start()

    ld_r.wait()
    mine = (picked // 2 == d).astype(F32)
    odd = (picked % 2).astype(F32)
    for k in range(4):
        r0 = RQ[0, 64 * k : 64 * k + 64].astype(F32)
        r1 = RQ[1, 64 * k : 64 * k + 64].astype(F32)
        RX[k] = (r0 * (1.0 - odd) + r1 * odd) * mine
    r_x = []
    for k in (1, 2, 3):
        cp = rcopy(RX.at[(gx + k) % 4], RX.at[3 + k], rs.at[k - 1], rr.at[k - 1], xs[k - 1])
        cp.start()
        r_x.append(cp)

    def shifted(ref, at, y):
        t = [ref[at + (rows_at(PAD + y - T),)], ref[at + (rows_at(PAD + y),)]]
        for i in range(1, G // T + 1):
            t.append(ref[at + (rows_at(PAD + y + T * i),)])
            after = pltpu.roll(jnp.where(sub == 0, t[i + 1], t[i]), T - 1, 0)
            before = pltpu.roll(jnp.where(sub == T - 1, t[i - 1], t[i]), 1, 0)
            yield t[i], after, before

    def coef(p, y):
        for i, (b, after, before) in enumerate(shifted(B, (p + 3,), y)):
            sl, at = rows_at(y + T * i), rows_at(PAD + y + T * i)
            xp, xm = B[p + 4, at], B[p + 2, at]
            zn = jnp.where(lane == 255, 0.0, pltpu.roll(b, 255, 1))
            zp = jnp.where(lane == 0, 0.0, pltpu.roll(b, 1, 1))
            CX[p + 3, sl] = 0.5 * (b + xp)
            CX[p + 2, sl] = 0.5 * (b + xm)
            CYP[p + 2, sl] = 0.5 * (b + after)
            CYM[p + 2, sl] = 0.5 * (b + before)
            CZP[p + 2, sl] = jnp.where(lane == 255, 0.0, 0.5 * (b + zn))
            CZM[p + 2, sl] = jnp.where(lane == 0, 0.0, 0.5 * (b + zp))
            DG[p + 2, sl] = 3.0 * b + 0.5 * ((xp + xm) + (after + before) + (zn + zp))

    planes(6, lambda i, y: coef(i + 1, y))

    def laps(k, p, y):
        for i, (v, after, before) in enumerate(shifted(U, (k, p + 3), y)):
            sl, at = rows_at(y + T * i), rows_at(PAD + y + T * i)
            t = CX[p + 3, sl] * U[k, p + 4, at] + CX[p + 2, sl] * U[k, p + 2, at]
            t = t + (CYP[p + 2, sl] * after + CYM[p + 2, sl] * before)
            t = t + (CZP[p + 2, sl] * pltpu.roll(v, 255, 1) + CZM[p + 2, sl] * pltpu.roll(v, 1, 1))
            yield sl, at, v, t - DG[p + 2, sl] * v

    def first_lap(p, y):
        for sl, _, _, t in laps(0, p, y):
            LU[0, p + 3, sl] = t

    planes(6, lambda i, y: first_lap(i + 1, y))

    d_l.wait()
    d_r.wait()
    near_d = jnp.concatenate([DH[0, 5:8], DS[...], DH[1, 0:3], jnp.zeros((2, 128), F32)], axis=0)
    rolled = [near_d if y == 0 else pltpu.roll(near_d, (-y) % 128, 1) for y in range(-3, 4)]
    key = jnp.transpose(jnp.concatenate(rolled + [jnp.zeros((16, 128), F32)], axis=0))
    for p in range(14):
        DB[p] = jnp.broadcast_to(key[:, 48 + p : 49 + p], (128, 128))
    KEY[...] = key
    idx = jnp.dot(key.astype(jnp.bfloat16), pick[...], preferred_element_type=F32) + shift[0:1, :]
    idx = jnp.clip(idx, 0.0, 255.0).astype(I32)
    for q in range(4):
        IDX[q] = idx[:, 128 * q : 128 * q + 128]
    SIDX[...] = idx[:, 512:640]

    def take(v, i):
        return jnp.take_along_axis(v, i, axis=1, mode="promise_in_bounds")

    def compact(which, read, heights, spare=None):
        def body(t):
            halves = []
            for half in range(2):
                i = SIDX[pl.ds(pl.multiple_of(64 * half + T * t, T), T)]
                low, i = i < 128, i & 127
                for side in range(2):
                    for h in heights:
                        v = read(7 - h if side else h, 64 * half + T * t)
                        g = jnp.where(low, take(v[:, :128], i), take(v[:, 128:], i))
                        start = 64 * side + STARTS[h]
                        out = g if side == 0 and h == heights[0] else jnp.where(lane1 >= start, g, out)
                    if spare is not None:
                        v = spare(6 if side else 1, 64 * half + T * t)
                        g = jnp.where(low, take(v[:, :128], i), take(v[:, 128:], i))
                        out = jnp.where(lane1 == 64 * side + SPARE, g, out)
                halves.append(out)
            a, b = halves
            SG[which, 0, t] = jnp.where(lane1 < 64, a, pltpu.roll(b, 64, 1))
            SG[which, 1, t] = jnp.where(lane1 < 64, pltpu.roll(a, 64, 1), b)

        loop(8, body, 4)
        a = rcopy(SG.at[which, 0], RG.at[which, 1], hs.at[which, 0], hr.at[which, 0], left)
        b = rcopy(SG.at[which, 1], RG.at[which, 0], hs.at[which, 1], hr.at[which, 1], right)
        a.start()
        b.start()
        return a, b

    def at_ends(do):
        @pl.when(d == 0)
        def _():
            do(0)

        @pl.when(d == 31)
        def _():
            do(1)

    def expand(which, cps, write, heights):
        for cp in cps:
            cp.wait()

        def blank(side):
            for t in range(8):
                RG[which, side, t] = jnp.zeros((T, 128), F32)

        at_ends(blank)

        def body(t):
            for side in range(2):
                v = RG[which, side, t % 8]
                for h in heights:
                    i = INVH[3 * side + h, t]
                    g = jnp.concatenate([take(v, i[:, :128]), take(v, i[:, 128:])], axis=1)
                    write(8 + h if side else -1 - h, T * t, g)

        loop(16, body, 4)

    h_b = compact(
        0, lambda p, y: B[p + 3, rows_at(PAD + y)], (1, 2), lambda p, y: U[0, p + 3, rows_at(PAD + y)]
    )

    ups = [bands(across(h + 1), STARTS[h]) for h in range(3)]
    downs = [{(7 - p, y): v for (p, y), v in band.items()} for band in ups]

    def mark(invs, maps, cells):
        for p, y in sorted(set().union(*maps)):
            col = 16 * (y + 3) + p + 3
            off = lane_f - cells[:, col : col + 1]
            dist = jnp.abs(off)
            for i, band in enumerate(maps):
                if (p, y) in band:
                    w, base = band[p, y]
                    invs[i] = jnp.where(dist <= w, off + (base + w), invs[i])
        return invs

    def invert_halo(t):
        cells = KEY[rows_at(T * t)]
        for side, maps in enumerate((ups, downs)):
            invs = mark([jnp.zeros((T, 256), F32)] * 3, maps, cells)
            for h in range(3):
                INVH[3 * side + h, t] = invs[h].astype(I32) + 64 * (t // 8)

    loop(16, invert_halo, 2)

    def invert(t):
        cells = KEY[rows_at(32 * s + T * t)]
        maps = [bands(near(x), 64 * (x % 2)) for x in range(8)]
        invs = mark([jnp.full((T, 256), -1.0, F32)] * 8, maps, cells)
        for x in range(8):
            INV[x, t] = invs[x].astype(I32)

    loop(4, invert)

    other = 2 * (1 - zl) + c
    p_f = [rcopy(PG.at[other, f], PG.at[other, f], ps.at[2, f], pr.at[2, f], core) for f in range(2)]
    for f in range(2):
        p_z[f].wait_recv()
        p_f[f].start()

    for cp in r_x:
        cp.wait()
    for k in range(4):
        sl = pl.ds(16 * k, 16)
        RY[k] = RX[gx, sl] + RX[4, sl] + RX[5, sl] + RX[6, sl]
    r_y = []
    for k in (1, 2, 3):
        cp = rcopy(RY.at[(gy + k) % 4], RY.at[3 + k], rs.at[2 + k], rr.at[2 + k], ys[k - 1])
        cp.start()
        r_y.append(cp)

    e_l.wait()
    e_r.wait()
    for e, p in enumerate((-1, 8)):
        for j in range(8):
            sl = slice(16 * j, 16 * j + 16)
            at = slice(PAD + 16 * j, PAD + 16 * j + 16)
            U[0, p + 3, at] = RE[e, 0, sl].astype(I32).astype(F32) * (1.0 / USCALE)
            B[p + 3, at] = RE[e, 1, sl].astype(I32).astype(F32) * (1.0 / BSCALE) + 1.0

    def no_edge(side):
        for j in range(16):
            U[0, 11 if side else 2, padded(j)] = zero
            B[11 if side else 2, padded(j)] = zero

    at_ends(no_edge)
    planes(2, lambda i, y: coef(7 * i, y))
    planes(2, lambda i, y: first_lap(7 * i, y))
    ld_base.wait()
    ld_lat.wait()
    ld_sb.wait()
    p_c.wait()
    for f in range(2):
        p_f[f].wait()
        p_z[f].wait_send()

    first = d * 8

    def pulse(n, p):
        return jnp.where(first + p == cell_x, wav[n, picked], 0.0)

    def step_one(p, y):
        factor = pulse(0, p)
        for i in range(G // 16):
            sl, at = rows_at(y + 16 * i, 16), rows_at(PAD + y + 16 * i, 16)
            k, o = i // 2, slice(16 * (i % 2), 16 * (i % 2) + 16)
            g = PG[k, 0, p, o].astype(F32)
            b = PG[k, 1, p, o].astype(F32)
            sq = jnp.tanh(LAT[p, sl] * g + b)
            m = BASE[p, sl] * jnp.exp(0.25 * sq)
            M[p + 3, sl] = m
            Q[p, sl] = m * 0.25 * (1.0 - sq * sq)
            new = 2.0 * U[0, p + 3, at] - SB[p, sl] + m * LU[0, p + 3, sl]
            U[1, p + 3, at] = new + factor * HIT[sl]

    planes(6, lambda i, y: step_one(i + 2 * (i // 3), y))
    h_u = compact(1, lambda p, y: U[1, p + 3, rows_at(PAD + y)], (0, 1, 2))
    h_m = compact(2, lambda p, y: M[p + 3, rows_at(y)], (0, 1, 2))
    planes(2, lambda i, y: step_one(i + 3, y))

    for cp in r_y:
        cp.wait()
    for k in range(2):
        sl = pl.ds(8 * k, 8)
        RZ[k] = RY[gy, sl] + RY[4, sl] + RY[5, sl] + RY[6, sl]
    r_z = rcopy(RZ.at[1 - gz], RZ.at[2], rs.at[6], rr.at[6], zs)
    r_z.start()

    def write_b(p, y, g):
        B[p + 3, rows_at(PAD + y)] = g

    expand(0, h_b, write_b, (1, 2))

    def second(t):
        slot = jnp.full((T, 128), SPARE, I32) + 64 * (t // 8)
        for side in range(2):
            U[0, 12 if side else 1, rows_at(PAD + T * t)] = twice(take(RG[0, side, t % 8], slot))

    loop(16, second, 4)
    planes(4, lambda i, y: coef(i - 2 + 8 * (i // 2), y))

    r_z.wait()
    RALL[s] = RZ[gz] + RZ[2]
    r_s = []
    for i, p in enumerate((core, zlo, far)):
        cp = rcopy(RALL.at[s], RALL.at[s], rs.at[7 + i], rr.at[7 + i], p)
        cp.start()
        r_s.append(cp)

    def advance(n, p):
        factor = pulse(n, p)
        for sl, at, v, a in laps(n, p, 0):
            m = M[p + 3, sl]
            LU[n, p + 3, sl] = a
            new = 2.0 * v - U[n - 1, p + 3, at] + m * a + factor * HIT[sl]
            r = jnp.where(lane_f == twice(DB[p + 3, sl]), new - twice(RB[n, p + 3, sl]), 0.0)
            AA[n, p + 3, sl] = r
            yield sl, at, m, new, r

    def step(n, p, y):
        for _, at, _, new, _ in advance(n, p):
            U[n + 1, p + 3, at] = new

    def last_step(p, y):
        for _, at, m, _, r in advance(3, p):
            U[0, p + 3, at] = m * r

    for cp in r_s:
        cp.wait()
    rt = jnp.transpose(jnp.concatenate([RALL[k] for k in range(4)] + [jnp.zeros((96, 128), F32)], axis=0))
    for k in range(4):
        for x in range(8):
            RB[k, x + 3] = jnp.broadcast_to(rt[:, 8 * k + x : 8 * k + x + 1], (128, 128))

    def inside(t, _):
        planes(6 - 2 * t, lambda i, y: step(1 + t, 1 + t + i, y))
        return 0

    lax.fori_loop(0, 2, inside, 0)
    planes(2, lambda i, y: last_step(3 + i, y))

    def write_u(p, y, g):
        U[1, p + 3, rows_at(PAD + y)] = g

    def write_m(p, y, g):
        M[p + 3, rows_at(y)] = g

    expand(1, h_u, write_u, (0, 1, 2))

    expand(2, h_m, write_m, (0, 1, 2))

    def outside(t, _):
        planes(6, lambda i, y: step(1 + t, t - 2 + i + (6 - 2 * t) * (i // 3), y))
        return 0

    lax.fori_loop(0, 2, outside, 0)
    planes(6, lambda i, y: last_step(i + 2 * (i // 3), y))

    sends = [(3, 0), (3, 1), (3, 2), (2, 0), (2, 1), (1, 0)]

    def pack(t):
        at = rows_at(T * t)
        out = jnp.zeros((T, 128), F32)
        for side in range(2):
            for i, (k, h) in enumerate(sends):
                total = jnp.sum(AA[k, 3 + (7 - h if side else h), at], axis=1, keepdims=True)
                out = jnp.where(lane1 == 8 * side + i, total, out)
        KT[at] = out

    loop(16, pack, 4)
    packed = jnp.transpose(KT[...])
    SR[0] = packed[0:8]
    SR[1] = packed[8:16]
    r_l = rcopy(SR.at[0], RR.at[1], ds_.at[2], dr_.at[2], left)
    r_r = rcopy(SR.at[1], RR.at[0], ds_.at[3], dr_.at[3], right)
    r_l.start()
    r_r.start()

    def back(k, p, y):
        for sl, at, _, t in laps(3 - k, p, y):
            a = AA[k - 1, p + 3, sl] + t + 2.0 * AA[k, p + 3, sl] - AA[k + 1, p + 3, sl]
            AA[k - 1, p + 3, sl] = a
            U[4 - k, p + 3, at] = M[p + 3, sl] * a

    def finish(p, y):
        for sl, at, _, t in laps(2, p, y):
            a2, a3 = AA[1, p + 3, sl], AA[2, p + 3, sl]
            a1 = AA[0, p + 3, sl] + t + 2.0 * a2 - a3
            img = AA[3, p + 3, sl] * LU[3, p + 3, sl] + a3 * LU[2, p + 3, sl]
            img = img + a2 * LU[1, p + 3, sl] + a1 * LU[0, p + 3, sl]
            IMG[p, sl] = img
            com = img * Q[p, sl]
            CB[p, sl] = com
            CA[p, sl] = com * LAT[p, sl]

    def resid_one(p, y):
        for i in range(G // T):
            sl = rows_at(y + T * i)
            r = U[1, p + 3, rows_at(PAD + y + T * i)] - twice(RB[0, p + 3, sl])
            AA[0, p + 3, sl] = jnp.where(lane_f == twice(DB[p + 3, sl]), r, 0.0)

    planes(8, resid_one)

    def inside_back(t, _):
        planes(6 - 2 * t, lambda i, y: back(3 - t, 1 + t + i, y))
        return 0

    lax.fori_loop(0, 2, inside_back, 0)
    planes(2, lambda i, y: finish(3 + i, y))

    r_l.wait()
    r_r.wait()

    def no_resid(side):
        RR[side] = jnp.zeros((8, 128), F32)

    at_ends(no_resid)
    KT[...] = jnp.transpose(jnp.concatenate([RR[0], RR[1], jnp.zeros((112, 128), F32)], axis=0))
    for side in range(2):
        for i, (k, h) in enumerate(sends):
            p = 8 + h if side else -1 - h
            for j in range(16):
                sl = tile(j)
                col = 8 * side + i
                r = jnp.where(lane_f == twice(DB[p + 3, sl]), KT[sl, col : col + 1], 0.0)
                AA[k, p + 3, sl] = r
                if k == 3:
                    U[0, p + 3, padded(j)] = M[p + 3, sl] * r

    def outside_back(t, _):
        planes(6, lambda i, y: back(3 - t, t - 2 + i + (6 - 2 * t) * (i // 3), y))
        return 0

    lax.fori_loop(0, 2, outside_back, 0)

    pair = 2 * (1 - zl) + c

    def core_copy(i, q):
        return rcopy(CG.at[2 * i + (1 - c), q], RA.at[i, q], gs.at[i, q], gr.at[i, q], core)

    def zlo_copy(q):
        return rcopy(CG.at[pair, q], RBUF.at[q], gs.at[2, q], gr.at[2, q], zlo)

    def compact_grads(q):
        def body(t):
            k, u = (s + 1 + t // 4) % 4, t % 4
            at = rows_at(32 * k + T * u)
            i = IDX[q, at]
            low, i = i < 128, i & 127
            for f, src in enumerate((CA, CB)):
                halves = []
                for x in range(2):
                    v = src[2 * q + x, at]
                    halves.append(jnp.where(low, take(v[:, :128], i), take(v[:, 128:], i)))
                CG[k, q, f, u] = jnp.where(lane1 < 64, halves[0], halves[1])

        loop(12, body, 4)

    def pass_on(q):
        core_copy(1 - zl, q).wait()
        for f in range(2):
            CG[pair, q, f] = CG[pair, q, f] + RA[1 - zl, q, f]
        zlo_copy(q).start()

    def begins(i):
        return 2 + 3 * i - 8 * (i // 2) + 3 * (i // 3)

    def stage(i):
        loop(1 + i // 2, lambda j: finish(begins(i) + j, 0))
        q = begins(i) // 2
        compact_grads(q)
        core_copy(1 - zl, q).start()
        core_copy(zl, q).start()

        @pl.when(i >= 1)
        def _():
            pass_on(begins(i - 1) // 2)

    loop(4, stage)
    out_i = load(0, IMG, img_h)
    pass_on(3)

    def out_copies(q):
        at = pl.ds(2 * q, 2)
        return [
            pltpu.make_async_copy(GA.at[at], gg_h.at[at], osem.at[0, q]),
            pltpu.make_async_copy(GB.at[at], bg_h.at[at], osem.at[1, q]),
        ]

    def last(i):
        q = begins(i) // 2
        core_copy(zl, q).wait()
        zlo_copy(q).wait()

        def spread(t):
            at, to = rows_at(32 * s + T * t), rows_at(T * t)
            for f, src, out in ((0, CA, GA), (1, CB, GB)):
                v = RA[zl, q, f, t] + RBUF[q, f, t]
                for x in range(2):
                    i = INV[2 * q + x, t]
                    have, i = i >= 0, i & 127
                    g = jnp.concatenate([take(v, i[:, :128]), take(v, i[:, 128:])], axis=1)
                    out[2 * q + x, to] = src[2 * q + x, at] + jnp.where(have, g, 0.0)

        loop(4, spread, 2)
        for cp in out_copies(q):
            cp.start()

    loop(4, last)
    out_i.wait()
    for q in range(4):
        for cp in out_copies(q):
            cp.wait()


def hand_out(img, gg, bg, img_o, gg_o, bg_o, vi, vg, vb, sem):
    moves = [(img.at[p], vi.at[p], img_o.at[p]) for p in range(8)] + [(gg, vg, gg_o), (bg, vb, bg_o)]
    come = [pltpu.make_async_copy(a, b, sem.at[0, i]) for i, (a, b, _) in enumerate(moves)]
    go = [pltpu.make_async_copy(b, o, sem.at[1, i]) for i, (_, b, o) in enumerate(moves)]
    for cp in come:
        cp.start()
    for a, b in zip(come, go):
        a.wait()
        b.start()
    for cp in go:
        cp.wait()


def shards(
    state_before, state_now, base_model, buoyancy, latent, flow_gain, flow_bias, records, source_wavelet, source_cell,
    shot, receiver_depth,
):
    any_ = pl.BlockSpec(memory_space=pl.ANY)
    smem = pl.BlockSpec(memory_space=pltpu.SMEM)
    vmem = pl.BlockSpec(memory_space=pltpu.VMEM)
    field = (8, 128, 256)
    halo = (14, 144, 256)
    pick, shift = tables()
    results = (
        jax.ShapeDtypeStruct(field, F32),
        jax.ShapeDtypeStruct((8, 32, 256), F32),
        jax.ShapeDtypeStruct((8, 32, 256), F32),
    )
    made = pl.pallas_call(
        kernel,
        out_shape=results,
        in_specs=[any_] * 8 + [smem] * 3 + [vmem] * 3,
        out_specs=(any_, any_, any_),
        scratch_shapes=[
            pltpu.VMEM((4,) + halo, F32),
            pltpu.VMEM(halo, F32),
            pltpu.VMEM(field, F32),
            pltpu.VMEM(field, F32),
            pltpu.VMEM(field, F32),
            pltpu.VMEM((4, 2, 8, 32, 256), jnp.bfloat16),
            pltpu.VMEM((2, 256, 128), jnp.bfloat16),
            pltpu.VMEM((4, 14, 128, 256), F32),
            pltpu.VMEM((5, 14, 128, 256), F32),
            pltpu.VMEM((14, 128, 256), F32),
            pltpu.VMEM(field, F32),
            pltpu.VMEM((13, 128, 256), F32),
            pltpu.VMEM((12, 128, 256), F32),
            pltpu.VMEM((12, 128, 256), F32),
            pltpu.VMEM((12, 128, 256), F32),
            pltpu.VMEM((12, 128, 256), F32),
            pltpu.VMEM((12, 128, 256), F32),
            pltpu.VMEM((14, 128, 128), F32),
            pltpu.VMEM((4, 14, 128, 128), F32),
            pltpu.VMEM((128, 128), F32),
            pltpu.VMEM((128, 256), F32),
            pltpu.VMEM(field, F32),
            pltpu.VMEM(field, F32),
            pltpu.VMEM(field, F32),
            pltpu.VMEM((8, 32, 256), F32),
            pltpu.VMEM((8, 32, 256), F32),
            pltpu.VMEM((4, 4, 2, 4, 8, 128), F32),
            pltpu.VMEM((2, 4, 2, 4, 8, 128), F32),
            pltpu.VMEM((4, 2, 4, 8, 128), F32),
            pltpu.VMEM((7, 64, 128), F32),
            pltpu.VMEM((7, 16, 128), F32),
            pltpu.VMEM((3, 8, 128), F32),
            pltpu.VMEM((4, 8, 128), F32),
            pltpu.VMEM((8, 128), F32),
            pltpu.VMEM((2, 8, 128), F32),
            pltpu.VMEM((4, 128, 128), I32),
            pltpu.VMEM((8, 4, 8, 256), I32),
            pltpu.VMEM((128, 128), I32),
            pltpu.VMEM((6, 16, 8, 256), I32),
            pltpu.VMEM((2, 2, 128, 256), jnp.int16),
            pltpu.VMEM((2, 2, 128, 256), jnp.int16),
            pltpu.VMEM((3, 2, 8, 8, 128), F32),
            pltpu.VMEM((3, 2, 8, 8, 128), F32),
            pltpu.VMEM((128, 128), F32),
            pltpu.VMEM((2, 8, 128), F32),
            pltpu.VMEM((2, 8, 128), F32),
            pltpu.SemaphoreType.DMA((8,)),
            pltpu.SemaphoreType.DMA((2, 4)),
            pltpu.SemaphoreType.DMA((2,)),
            pltpu.SemaphoreType.DMA((2,)),
            pltpu.SemaphoreType.DMA((3, 2)),
            pltpu.SemaphoreType.DMA((3, 2)),
            pltpu.SemaphoreType.DMA((3, 2)),
            pltpu.SemaphoreType.DMA((3, 2)),
            pltpu.SemaphoreType.DMA((3, 4)),
            pltpu.SemaphoreType.DMA((3, 4)),
            pltpu.SemaphoreType.DMA((10,)),
            pltpu.SemaphoreType.DMA((10,)),
            pltpu.SemaphoreType.DMA((4,)),
            pltpu.SemaphoreType.DMA((4,)),
        ],
        compiler_params=pltpu.CompilerParams(
            collective_id=1, has_side_effects=True, vmem_limit_bytes=58 << 20
        ),
        name="flow_gradient",
    )(
        state_before[0], state_now[0], base_model, buoyancy, latent[0], flow_gain, flow_bias, records, source_wavelet.T,
        source_cell, shot, receiver_depth, jnp.asarray(pick, jnp.bfloat16), jnp.asarray(shift),
    )
    img, gg, bg = pl.pallas_call(
        hand_out,
        out_shape=results,
        in_specs=[any_] * 3,
        out_specs=(any_,) * 3,
        scratch_shapes=[pltpu.VMEM(r.shape, F32) for r in results] + [pltpu.SemaphoreType.DMA((2, 10))],
        name="hand_out",
    )(*made)
    return img[None], gg, bg


def solution(mesh):
    in_specs = (
        P("smp", "dom", None, None),
        P("smp", "dom", None, None),
        P("dom", None, None),
        P("dom", None, None),
        P("smp", "dom", None, None),
        P("dom", "smp", None),
        P("dom", "smp", None),
        P("dom", None, None, None),
        P(),
        P(),
        P(),
        P("dom", None),
    )
    out_specs = (P("smp", "dom", None, None), P("dom", "smp", None), P("dom", "smp", None))
    return jax.shard_map(shards, mesh=mesh, in_specs=in_specs, out_specs=out_specs, check_vma=False)
```

```python
import functools

import jax
import jax.numpy as jnp
import numpy as np
from jax import lax
from jax.experimental import pallas as pl
from jax.experimental.pallas import tpu as pltpu
from jax.sharding import PartitionSpec as P

MESH = pl.DeviceIdType.MESH
I32 = jnp.int32


def ball(radius):
    return [(a, b) for a in range(-radius, radius + 1) for b in range(abs(a) - radius, radius - abs(a) + 1)]


def near(plane):
    return [(plane + a, y, z) for a in range(-3, 4) for y, z in ball(3 - abs(a))]


def across(height):
    radius = {1: {0: 2, -1: 2, 1: 1, -2: 1, 2: 0, -3: 0}, 2: {0: 1, -1: 1, -2: 1, 1: 0, -3: 0}, 3: {0: 0, -2: 0, -3: 0}}
    return [(p, y, z) for p, r in radius[height].items() for y, z in ball(r)]


COUNTS = [len(across(h)) for h in (1, 2, 3)]
STARTS = [sum(COUNTS[:h]) for h in range(4)]


SPARE = 58
USCALE = 32767.0 / 6.0
BSCALE = 65532.0


def bands(cells, base=0):
    out = {}
    for i, (p, y, z) in enumerate(cells):
        w, first = out.get((p, y), (0, base + i))
        out[p, y] = (max(w, abs(z)), first)
    return out


def tables():
    up = sum((across(h) for h in (1, 2, 3)), [])
    down = [(-1 - p, y, z) for p, y, z in up]
    right = [[(p + 8, y, z) for p, y, z in cells] for cells in (up, down)]
    lists = [near(x) for x in range(8)] + [down, right[0]]
    pick = np.zeros((128, 64 * len(lists)), np.float32)
    shift = np.zeros((8, 64 * len(lists)), np.float32)
    for i, cells in enumerate(lists):
        if i >= 8:
            cells = cells + [{8: (-1, 0, 0), 9: (8, 0, 0)}[i]]
        cells = cells + [cells[0]] * (64 - len(cells))
        for j, (p, y, z) in enumerate(cells):
            pick[16 * (y + 3) + p + 3, 64 * i + j] = 1.0
            shift[:, 64 * i + j] = z
    return pick, shift


F32 = jnp.float32
PAD = 8
T = 8
G = 128


def kernel(
    sb_h, sn_h, base_h, buoy_h, lat_h, gain_h, bias_h, rec_h, wav, cell, shot, depth, pick, shift,
    img_h, gg_h, bg_h,
    U, B, SB, BASE, LAT, PG, RQ, LU, AA, M, Q, CX, CYP, CYM, CZP, CZM, DG, DB, RB, KEY, HIT, IMG, CA, CB, GA, GB, CG, RA, RBUF,
    RX, RY, RZ, RALL, DS, DH, IDX, INV, SIDX, INVH, SE, RE, SG, RG, KT, SR, RR,
    lsem, osem, es, er, hs, hr, ps, pr, gs, gr, rs, rr, ds_, dr_,
):
    d = lax.axis_index("dom")
    s = lax.axis_index("smp")
    gx, gy, gz = d // 8, (d // 2) % 4, d % 2
    zl, c = s // 2, s % 2
    left, right = ((d + 31) % 32, s), ((d + 1) % 32, s)
    core = (d, 2 * zl + (1 - c))
    zlo = (d, 2 * (1 - zl) + c)
    far = (d, 2 * (1 - zl) + (1 - c))
    xs = [(((gx + k) % 4) * 8 + d % 8, s) for k in (1, 2, 3)]
    ys = [(gx * 8 + ((gy + k) % 4) * 2 + gz, s) for k in (1, 2, 3)]
    zs = (d - gz + (1 - gz), s)

    def load(i, src, dst):
        cp = pltpu.make_async_copy(src, dst, lsem.at[i])
        cp.start()
        return cp

    rows = pl.ds(PAD, 128)
    own = pl.ds(3, 8)
    ld_g = load(2, gain_h, PG.at[s, 0])
    ld_c = load(3, bias_h, PG.at[s, 1])
    ld_u = load(0, sn_h, U.at[0, own, rows])
    ld_b = load(1, buoy_h, B.at[own, rows])
    ld_r = load(4, rec_h.at[:, s], RQ)
    ld_base = load(5, base_h, BASE)
    ld_lat = load(6, lat_h, LAT)
    ld_sb = load(7, sb_h, SB)

    barrier = pltpu.get_barrier_semaphore()
    peers = [left, right, core, zlo, far] + xs + ys
    for p in peers:
        pl.semaphore_signal(barrier, inc=1, device_id=p, device_id_type=MESH)

    def rcopy(src, dst, ss, sr, dev):
        return pltpu.make_async_remote_copy(
            src_ref=src, dst_ref=dst, send_sem=ss, recv_sem=sr, device_id=dev, device_id_type=MESH
        )

    def loop(n, body, per=1):
        def run(i, _):
            for k in range(per):
                body(i * per + k if per > 1 else i)
            return 0

        lax.fori_loop(0, n // per, run, 0)

    def rows_at(first, n=T):
        if isinstance(first, int):
            return slice(first, first + n)
        return pl.ds(pl.multiple_of(first, T), n)

    def planes(n, body):
        loop(n, lambda i: body(i, 0))

    zero = jnp.zeros((T, 256), F32)
    lane = lax.broadcasted_iota(I32, (T, 256), 1)
    lane1 = lax.broadcasted_iota(I32, (T, 128), 1)
    lane_f = lane.astype(F32)
    sub = lax.broadcasted_iota(I32, (T, 256), 0)

    def tile(j):
        return slice(T * j, T * j + T)

    def padded(j):
        return slice(PAD + T * j, PAD + T * j + T)

    def twice(v):
        return jnp.concatenate([v, v], axis=1)

    def clear(i):
        for n in range(4):
            U[n, i, 0:8] = zero
            U[n, i, 136:144] = zero
        B[i, 0:8] = zero
        B[i, 136:144] = zero
        for j in range(16):
            AA[4, i, tile(j)] = zero

    loop(14, clear)

    picked = shot[0]
    flat = cell[picked]
    cell_x = flat // (128 * 256)
    cell_y = (flat // 256) % 128
    cell_z = flat % 256
    for j in range(16):
        HIT[tile(j)] = jnp.where((sub + T * j == cell_y) & (lane == cell_z), 1.0, 0.0)
    DS[...] = depth[...].astype(F32)

    ld_u.wait()
    ld_b.wait()
    for e, p in enumerate((0, 7)):
        for j in range(8):
            sl = slice(16 * j, 16 * j + 16)
            at = slice(PAD + 16 * j, PAD + 16 * j + 16)
            SE[e, 0, sl] = jnp.round(U[0, p + 3, at] * USCALE).astype(I32).astype(jnp.int16)
            SE[e, 1, sl] = jnp.round((B[p + 3, at] - 1.0) * BSCALE).astype(I32).astype(jnp.int16)

    ld_g.wait()
    ld_c.wait()
    pl.semaphore_wait(barrier, len(peers))

    d_l = rcopy(DS, DH.at[1], ds_.at[0], dr_.at[0], left)
    d_r = rcopy(DS, DH.at[0], ds_.at[1], dr_.at[1], right)
    d_l.start()
    d_r.start()
    p_z = [rcopy(PG.at[s, f], PG.at[s, f], ps.at[0, f], pr.at[0, f], zlo) for f in range(2)]
    p_c = rcopy(PG.at[s], PG.at[s], ps.at[1, 0], pr.at[1, 0], core)
    p_z[0].start()
    p_z[1].start()
    e_l = rcopy(SE.at[0], RE.at[1], es.at[0], er.at[0], left)
    e_r = rcopy(SE.at[1], RE.at[0], es.at[1], er.at[1], right)
    e_l.start()
    e_r.start()
    p_c.start()

    ld_r.wait()
    mine = (picked // 2 == d).astype(F32)
    odd = (picked % 2).astype(F32)
    for k in range(4):
        r0 = RQ[0, 64 * k : 64 * k + 64].astype(F32)
        r1 = RQ[1, 64 * k : 64 * k + 64].astype(F32)
        RX[k] = (r0 * (1.0 - odd) + r1 * odd) * mine
    r_x = []
    for k in (1, 2, 3):
        cp = rcopy(RX.at[(gx + k) % 4], RX.at[3 + k], rs.at[k - 1], rr.at[k - 1], xs[k - 1])
        cp.start()
        r_x.append(cp)

    def shifted(ref, at, y):
        t = [ref[at + (rows_at(PAD + y - T),)], ref[at + (rows_at(PAD + y),)]]
        for i in range(1, G // T + 1):
            t.append(ref[at + (rows_at(PAD + y + T * i),)])
            after = pltpu.roll(jnp.where(sub == 0, t[i + 1], t[i]), T - 1, 0)
            before = pltpu.roll(jnp.where(sub == T - 1, t[i - 1], t[i]), 1, 0)
            yield t[i], after, before

    def coef(p, y):
        for i, (b, after, before) in enumerate(shifted(B, (p + 3,), y)):
            sl, at = rows_at(y + T * i), rows_at(PAD + y + T * i)
            xp, xm = B[p + 4, at], B[p + 2, at]
            zn = jnp.where(lane == 255, 0.0, pltpu.roll(b, 255, 1))
            zp = jnp.where(lane == 0, 0.0, pltpu.roll(b, 1, 1))
            CX[p + 3, sl] = 0.5 * (b + xp)
            CX[p + 2, sl] = 0.5 * (b + xm)
            CYP[p + 2, sl] = 0.5 * (b + after)
            CYM[p + 2, sl] = 0.5 * (b + before)
            CZP[p + 2, sl] = jnp.where(lane == 255, 0.0, 0.5 * (b + zn))
            CZM[p + 2, sl] = jnp.where(lane == 0, 0.0, 0.5 * (b + zp))
            DG[p + 2, sl] = 3.0 * b + 0.5 * ((xp + xm) + (after + before) + (zn + zp))

    planes(6, lambda i, y: coef(i + 1, y))

    def laps(k, p, y):
        for i, (v, after, before) in enumerate(shifted(U, (k, p + 3), y)):
            sl, at = rows_at(y + T * i), rows_at(PAD + y + T * i)
            t = CX[p + 3, sl] * U[k, p + 4, at] + CX[p + 2, sl] * U[k, p + 2, at]
            t = t + (CYP[p + 2, sl] * after + CYM[p + 2, sl] * before)
            t = t + (CZP[p + 2, sl] * pltpu.roll(v, 255, 1) + CZM[p + 2, sl] * pltpu.roll(v, 1, 1))
            yield sl, at, v, t - DG[p + 2, sl] * v

    def first_lap(p, y):
        for sl, _, _, t in laps(0, p, y):
            LU[0, p + 3, sl] = t

    planes(6, lambda i, y: first_lap(i + 1, y))

    def model(k):
        def body(p):
            for i in range(2):
                sl, o = rows_at(32 * k + 16 * i, 16), slice(16 * i, 16 * i + 16)
                sq = jnp.tanh(LAT[p, sl] * PG[k, 0, p, o].astype(F32) + PG[k, 1, p, o].astype(F32))
                m = BASE[p, sl] * jnp.exp(0.25 * sq)
                M[p + 3, sl] = m
                Q[p, sl] = m * 0.25 * (1.0 - sq * sq)

        loop(8, body, 2)

    ld_base.wait()
    ld_lat.wait()
    model(s)
    p_c.wait()
    model(2 * zl + (1 - c))

    d_l.wait()
    d_r.wait()
    near_d = jnp.concatenate([DH[0, 5:8], DS[...], DH[1, 0:3], jnp.zeros((2, 128), F32)], axis=0)
    rolled = [near_d if y == 0 else pltpu.roll(near_d, (-y) % 128, 1) for y in range(-3, 4)]
    key = jnp.transpose(jnp.concatenate(rolled + [jnp.zeros((16, 128), F32)], axis=0))
    for p in range(14):
        DB[p] = jnp.broadcast_to(key[:, 48 + p : 49 + p], (128, 128))
    KEY[...] = key
    idx = jnp.dot(key.astype(jnp.bfloat16), pick[...], preferred_element_type=F32) + shift[0:1, :]
    idx = jnp.clip(idx, 0.0, 255.0).astype(I32)
    for q in range(4):
        IDX[q] = idx[:, 128 * q : 128 * q + 128]
    SIDX[...] = idx[:, 512:640]

    def take(v, i):
        return jnp.take_along_axis(v, i, axis=1, mode="promise_in_bounds")

    def compact(which, read, heights, spare=None):
        def body(t):
            halves = []
            for half in range(2):
                i = SIDX[pl.ds(pl.multiple_of(64 * half + T * t, T), T)]
                low, i = i < 128, i & 127
                for side in range(2):
                    for h in heights:
                        v = read(7 - h if side else h, 64 * half + T * t)
                        g = jnp.where(low, take(v[:, :128], i), take(v[:, 128:], i))
                        start = 64 * side + STARTS[h]
                        out = g if side == 0 and h == heights[0] else jnp.where(lane1 >= start, g, out)
                    if spare is not None:
                        v = spare(6 if side else 1, 64 * half + T * t)
                        g = jnp.where(low, take(v[:, :128], i), take(v[:, 128:], i))
                        out = jnp.where(lane1 == 64 * side + SPARE, g, out)
                halves.append(out)
            a, b = halves
            SG[which, 0, t] = jnp.where(lane1 < 64, a, pltpu.roll(b, 64, 1))
            SG[which, 1, t] = jnp.where(lane1 < 64, pltpu.roll(a, 64, 1), b)

        loop(8, body, 4)
        a = rcopy(SG.at[which, 0], RG.at[which, 1], hs.at[which, 0], hr.at[which, 0], left)
        b = rcopy(SG.at[which, 1], RG.at[which, 0], hs.at[which, 1], hr.at[which, 1], right)
        a.start()
        b.start()
        return a, b

    def at_ends(do):
        @pl.when(d == 0)
        def _():
            do(0)

        @pl.when(d == 31)
        def _():
            do(1)

    def expand(which, cps, write, heights):
        for cp in cps:
            cp.wait()

        def blank(side):
            for t in range(8):
                RG[which, side, t] = jnp.zeros((T, 128), F32)

        at_ends(blank)

        def body(t):
            for side in range(2):
                v = RG[which, side, t % 8]
                for h in heights:
                    i = INVH[3 * side + h, t]
                    g = jnp.concatenate([take(v, i[:, :128]), take(v, i[:, 128:])], axis=1)
                    write(8 + h if side else -1 - h, T * t, g)

        loop(16, body, 4)

    h_b = compact(
        0, lambda p, y: B[p + 3, rows_at(PAD + y)], (1, 2), lambda p, y: U[0, p + 3, rows_at(PAD + y)]
    )

    ups = [bands(across(h + 1), STARTS[h]) for h in range(3)]
    downs = [{(7 - p, y): v for (p, y), v in band.items()} for band in ups]

    def mark(invs, maps, cells):
        for p, y in sorted(set().union(*maps)):
            col = 16 * (y + 3) + p + 3
            off = lane_f - cells[:, col : col + 1]
            dist = jnp.abs(off)
            for i, band in enumerate(maps):
                if (p, y) in band:
                    w, base = band[p, y]
                    invs[i] = jnp.where(dist <= w, off + (base + w), invs[i])
        return invs

    def invert_halo(t):
        cells = KEY[rows_at(T * t)]
        for side, maps in enumerate((ups, downs)):
            invs = mark([jnp.zeros((T, 256), F32)] * 3, maps, cells)
            for h in range(3):
                INVH[3 * side + h, t] = invs[h].astype(I32) + 64 * (t // 8)

    loop(16, invert_halo, 2)

    def invert(t):
        cells = KEY[rows_at(32 * s + T * t)]
        maps = [bands(near(x), 64 * (x % 2)) for x in range(8)]
        invs = mark([jnp.full((T, 256), -1.0, F32)] * 8, maps, cells)
        for x in range(8):
            INV[x, t] = invs[x].astype(I32)

    loop(4, invert)

    other = 2 * (1 - zl) + c
    p_f = [rcopy(PG.at[other, f], PG.at[other, f], ps.at[2, f], pr.at[2, f], core) for f in range(2)]
    for f in range(2):
        p_z[f].wait_recv()
        p_f[f].start()

    for cp in r_x:
        cp.wait()
    for k in range(4):
        sl = pl.ds(16 * k, 16)
        RY[k] = RX[gx, sl] + RX[4, sl] + RX[5, sl] + RX[6, sl]
    r_y = []
    for k in (1, 2, 3):
        cp = rcopy(RY.at[(gy + k) % 4], RY.at[3 + k], rs.at[2 + k], rr.at[2 + k], ys[k - 1])
        cp.start()
        r_y.append(cp)

    e_l.wait()
    e_r.wait()
    for e, p in enumerate((-1, 8)):
        for j in range(8):
            sl = slice(16 * j, 16 * j + 16)
            at = slice(PAD + 16 * j, PAD + 16 * j + 16)
            U[0, p + 3, at] = RE[e, 0, sl].astype(I32).astype(F32) * (1.0 / USCALE)
            B[p + 3, at] = RE[e, 1, sl].astype(I32).astype(F32) * (1.0 / BSCALE) + 1.0

    def no_edge(side):
        for j in range(16):
            U[0, 11 if side else 2, padded(j)] = zero
            B[11 if side else 2, padded(j)] = zero

    at_ends(no_edge)
    planes(2, lambda i, y: coef(7 * i, y))
    planes(2, lambda i, y: first_lap(7 * i, y))
    ld_sb.wait()
    model(other)
    for f in range(2):
        p_f[f].wait()
        p_z[f].wait_send()
    model(2 * (1 - zl) + (1 - c))

    first = d * 8

    def pulse(n, p):
        return jnp.where(first + p == cell_x, wav[n, picked], 0.0)

    def step_one(p, y):
        factor = pulse(0, p)
        for i in range(16):
            sl, at = rows_at(y + T * i), rows_at(PAD + y + T * i)
            new = 2.0 * U[0, p + 3, at] - SB[p, sl] + M[p + 3, sl] * LU[0, p + 3, sl]
            U[1, p + 3, at] = new + factor * HIT[sl]

    planes(6, lambda i, y: step_one(i + 2 * (i // 3), y))
    h_u = compact(1, lambda p, y: U[1, p + 3, rows_at(PAD + y)], (0, 1, 2))
    h_m = compact(2, lambda p, y: M[p + 3, rows_at(y)], (0, 1, 2))
    planes(2, lambda i, y: step_one(i + 3, y))

    for cp in r_y:
        cp.wait()
    for k in range(2):
        sl = pl.ds(8 * k, 8)
        RZ[k] = RY[gy, sl] + RY[4, sl] + RY[5, sl] + RY[6, sl]
    r_z = rcopy(RZ.at[1 - gz], RZ.at[2], rs.at[6], rr.at[6], zs)
    r_z.start()

    def write_b(p, y, g):
        B[p + 3, rows_at(PAD + y)] = g

    expand(0, h_b, write_b, (1, 2))

    def second(t):
        slot = jnp.full((T, 128), SPARE, I32) + 64 * (t // 8)
        for side in range(2):
            U[0, 12 if side else 1, rows_at(PAD + T * t)] = twice(take(RG[0, side, t % 8], slot))

    loop(16, second, 4)
    planes(4, lambda i, y: coef(i - 2 + 8 * (i // 2), y))

    r_z.wait()
    RALL[s] = RZ[gz] + RZ[2]
    r_s = []
    for i, p in enumerate((core, zlo, far)):
        cp = rcopy(RALL.at[s], RALL.at[s], rs.at[7 + i], rr.at[7 + i], p)
        cp.start()
        r_s.append(cp)

    def advance(n, p):
        factor = pulse(n, p)
        for sl, at, v, a in laps(n, p, 0):
            m = M[p + 3, sl]
            LU[n, p + 3, sl] = a
            new = 2.0 * v - U[n - 1, p + 3, at] + m * a + factor * HIT[sl]
            r = jnp.where(lane_f == twice(DB[p + 3, sl]), new - twice(RB[n, p + 3, sl]), 0.0)
            AA[n, p + 3, sl] = r
            yield sl, at, m, new, r

    def step(n, p, y):
        for _, at, _, new, _ in advance(n, p):
            U[n + 1, p + 3, at] = new

    def last_step(p, y):
        for _, at, m, _, r in advance(3, p):
            U[0, p + 3, at] = m * r

    for cp in r_s:
        cp.wait()
    rt = jnp.transpose(jnp.concatenate([RALL[k] for k in range(4)] + [jnp.zeros((96, 128), F32)], axis=0))
    for k in range(4):
        for x in range(8):
            RB[k, x + 3] = jnp.broadcast_to(rt[:, 8 * k + x : 8 * k + x + 1], (128, 128))

    def inside(t, _):
        planes(6 - 2 * t, lambda i, y: step(1 + t, 1 + t + i, y))
        return 0

    lax.fori_loop(0, 2, inside, 0)
    planes(2, lambda i, y: last_step(3 + i, y))

    def write_u(p, y, g):
        U[1, p + 3, rows_at(PAD + y)] = g

    def write_m(p, y, g):
        M[p + 3, rows_at(y)] = g

    expand(1, h_u, write_u, (0, 1, 2))

    expand(2, h_m, write_m, (0, 1, 2))

    def outside(t, _):
        planes(6, lambda i, y: step(1 + t, t - 2 + i + (6 - 2 * t) * (i // 3), y))
        return 0

    lax.fori_loop(0, 2, outside, 0)
    planes(6, lambda i, y: last_step(i + 2 * (i // 3), y))

    sends = [(3, 0), (3, 1), (3, 2), (2, 0), (2, 1), (1, 0)]

    def pack(t):
        at = rows_at(T * t)
        out = jnp.zeros((T, 128), F32)
        for side in range(2):
            for i, (k, h) in enumerate(sends):
                total = jnp.sum(AA[k, 3 + (7 - h if side else h), at], axis=1, keepdims=True)
                out = jnp.where(lane1 == 8 * side + i, total, out)
        KT[at] = out

    loop(16, pack, 4)
    packed = jnp.transpose(KT[...])
    SR[0] = packed[0:8]
    SR[1] = packed[8:16]
    r_l = rcopy(SR.at[0], RR.at[1], ds_.at[2], dr_.at[2], left)
    r_r = rcopy(SR.at[1], RR.at[0], ds_.at[3], dr_.at[3], right)
    r_l.start()
    r_r.start()

    def back(k, p, y):
        for sl, at, _, t in laps(3 - k, p, y):
            a = AA[k - 1, p + 3, sl] + t + 2.0 * AA[k, p + 3, sl] - AA[k + 1, p + 3, sl]
            AA[k - 1, p + 3, sl] = a
            U[4 - k, p + 3, at] = M[p + 3, sl] * a

    def finish(p, y):
        for sl, at, _, t in laps(2, p, y):
            a2, a3 = AA[1, p + 3, sl], AA[2, p + 3, sl]
            a1 = AA[0, p + 3, sl] + t + 2.0 * a2 - a3
            img = IMG[p, sl] + a3 * LU[2, p + 3, sl]
            img = img + a2 * LU[1, p + 3, sl] + a1 * LU[0, p + 3, sl]
            IMG[p, sl] = img
            com = img * Q[p, sl]
            CB[p, sl] = com
            CA[p, sl] = com * LAT[p, sl]

    def resid_one(p, y):
        for i in range(G // T):
            sl = rows_at(y + T * i)
            r = U[1, p + 3, rows_at(PAD + y + T * i)] - twice(RB[0, p + 3, sl])
            AA[0, p + 3, sl] = jnp.where(lane_f == twice(DB[p + 3, sl]), r, 0.0)
            IMG[p, sl] = AA[3, p + 3, sl] * LU[3, p + 3, sl]

    planes(8, resid_one)

    def inside_back(t, _):
        planes(6 - 2 * t, lambda i, y: back(3 - t, 1 + t + i, y))
        return 0

    lax.fori_loop(0, 2, inside_back, 0)
    planes(2, lambda i, y: finish(3 + i, y))

    r_l.wait()
    r_r.wait()

    def no_resid(side):
        RR[side] = jnp.zeros((8, 128), F32)

    at_ends(no_resid)
    KT[...] = jnp.transpose(jnp.concatenate([RR[0], RR[1], jnp.zeros((112, 128), F32)], axis=0))
    for side in range(2):
        for i, (k, h) in enumerate(sends):
            p = 8 + h if side else -1 - h
            for j in range(16):
                sl = tile(j)
                col = 8 * side + i
                r = jnp.where(lane_f == twice(DB[p + 3, sl]), KT[sl, col : col + 1], 0.0)
                AA[k, p + 3, sl] = r
                if k == 3:
                    U[0, p + 3, padded(j)] = M[p + 3, sl] * r

    def outside_back(t, _):
        planes(6, lambda i, y: back(3 - t, t - 2 + i + (6 - 2 * t) * (i // 3), y))
        return 0

    lax.fori_loop(0, 2, outside_back, 0)

    pair = 2 * (1 - zl) + c

    def core_copy(i, q):
        return rcopy(CG.at[2 * i + (1 - c), q], RA.at[i, q], gs.at[i, q], gr.at[i, q], core)

    def zlo_copy(q):
        return rcopy(CG.at[pair, q], RBUF.at[q], gs.at[2, q], gr.at[2, q], zlo)

    def compact_grads(q):
        def body(t):
            k, u = (s + 1 + t // 4) % 4, t % 4
            at = rows_at(32 * k + T * u)
            i = IDX[q, at]
            low, i = i < 128, i & 127
            for f, src in enumerate((CA, CB)):
                halves = []
                for x in range(2):
                    v = src[2 * q + x, at]
                    halves.append(jnp.where(low, take(v[:, :128], i), take(v[:, 128:], i)))
                CG[k, q, f, u] = jnp.where(lane1 < 64, halves[0], halves[1])

        loop(12, body, 4)

    def pass_on(q):
        core_copy(1 - zl, q).wait()
        for f in range(2):
            CG[pair, q, f] = CG[pair, q, f] + RA[1 - zl, q, f]
        zlo_copy(q).start()

    def begins(i):
        return 2 + 3 * i - 8 * (i // 2) + 3 * (i // 3)

    def stage(i):
        loop(1 + i // 2, lambda j: finish(begins(i) + j, 0))
        q = begins(i) // 2
        compact_grads(q)
        core_copy(1 - zl, q).start()
        core_copy(zl, q).start()

        @pl.when(i >= 1)
        def _():
            pass_on(begins(i - 1) // 2)

    loop(4, stage)
    out_i = load(0, IMG, img_h)
    pass_on(3)

    def out_copies(q):
        at = pl.ds(2 * q, 2)
        return [
            pltpu.make_async_copy(GA.at[at], gg_h.at[at], osem.at[0, q]),
            pltpu.make_async_copy(GB.at[at], bg_h.at[at], osem.at[1, q]),
        ]

    def last(i):
        q = begins(i) // 2
        core_copy(zl, q).wait()
        zlo_copy(q).wait()

        def spread(t):
            at, to = rows_at(32 * s + T * t), rows_at(T * t)
            for f, src, out in ((0, CA, GA), (1, CB, GB)):
                v = RA[zl, q, f, t] + RBUF[q, f, t]
                for x in range(2):
                    i = INV[2 * q + x, t]
                    have, i = i >= 0, i & 127
                    g = jnp.concatenate([take(v, i[:, :128]), take(v, i[:, 128:])], axis=1)
                    out[2 * q + x, to] = src[2 * q + x, at] + jnp.where(have, g, 0.0)

        loop(4, spread, 2)
        for cp in out_copies(q):
            cp.start()

    loop(4, last)
    out_i.wait()
    for q in range(4):
        for cp in out_copies(q):
            cp.wait()


def hand_out(img, gg, bg, img_o, gg_o, bg_o, vi, vg, vb, sem):
    moves = [(img.at[p], vi.at[p], img_o.at[p]) for p in range(8)] + [(gg, vg, gg_o), (bg, vb, bg_o)]
    come = [pltpu.make_async_copy(a, b, sem.at[0, i]) for i, (a, b, _) in enumerate(moves)]
    go = [pltpu.make_async_copy(b, o, sem.at[1, i]) for i, (_, b, o) in enumerate(moves)]
    for cp in come:
        cp.start()
    for a, b in zip(come, go):
        a.wait()
        b.start()
    for cp in go:
        cp.wait()


def shards(
    state_before, state_now, base_model, buoyancy, latent, flow_gain, flow_bias, records, source_wavelet, source_cell,
    shot, receiver_depth,
):
    any_ = pl.BlockSpec(memory_space=pl.ANY)
    smem = pl.BlockSpec(memory_space=pltpu.SMEM)
    vmem = pl.BlockSpec(memory_space=pltpu.VMEM)
    field = (8, 128, 256)
    halo = (14, 144, 256)
    pick, shift = tables()
    results = (
        jax.ShapeDtypeStruct(field, F32),
        jax.ShapeDtypeStruct((8, 32, 256), F32),
        jax.ShapeDtypeStruct((8, 32, 256), F32),
    )
    made = pl.pallas_call(
        kernel,
        out_shape=results,
        in_specs=[any_] * 8 + [smem] * 3 + [vmem] * 3,
        out_specs=(any_, any_, any_),
        scratch_shapes=[
            pltpu.VMEM((4,) + halo, F32),
            pltpu.VMEM(halo, F32),
            pltpu.VMEM(field, F32),
            pltpu.VMEM(field, F32),
            pltpu.VMEM(field, F32),
            pltpu.VMEM((4, 2, 8, 32, 256), jnp.bfloat16),
            pltpu.VMEM((2, 256, 128), jnp.bfloat16),
            pltpu.VMEM((4, 14, 128, 256), F32),
            pltpu.VMEM((5, 14, 128, 256), F32),
            pltpu.VMEM((14, 128, 256), F32),
            pltpu.VMEM(field, F32),
            pltpu.VMEM((13, 128, 256), F32),
            pltpu.VMEM((12, 128, 256), F32),
            pltpu.VMEM((12, 128, 256), F32),
            pltpu.VMEM((12, 128, 256), F32),
            pltpu.VMEM((12, 128, 256), F32),
            pltpu.VMEM((12, 128, 256), F32),
            pltpu.VMEM((14, 128, 128), F32),
            pltpu.VMEM((4, 14, 128, 128), F32),
            pltpu.VMEM((128, 128), F32),
            pltpu.VMEM((128, 256), F32),
            pltpu.VMEM(field, F32),
            pltpu.VMEM(field, F32),
            pltpu.VMEM(field, F32),
            pltpu.VMEM((8, 32, 256), F32),
            pltpu.VMEM((8, 32, 256), F32),
            pltpu.VMEM((4, 4, 2, 4, 8, 128), F32),
            pltpu.VMEM((2, 4, 2, 4, 8, 128), F32),
            pltpu.VMEM((4, 2, 4, 8, 128), F32),
            pltpu.VMEM((7, 64, 128), F32),
            pltpu.VMEM((7, 16, 128), F32),
            pltpu.VMEM((3, 8, 128), F32),
            pltpu.VMEM((4, 8, 128), F32),
            pltpu.VMEM((8, 128), F32),
            pltpu.VMEM((2, 8, 128), F32),
            pltpu.VMEM((4, 128, 128), I32),
            pltpu.VMEM((8, 4, 8, 256), I32),
            pltpu.VMEM((128, 128), I32),
            pltpu.VMEM((6, 16, 8, 256), I32),
            pltpu.VMEM((2, 2, 128, 256), jnp.int16),
            pltpu.VMEM((2, 2, 128, 256), jnp.int16),
            pltpu.VMEM((3, 2, 8, 8, 128), F32),
            pltpu.VMEM((3, 2, 8, 8, 128), F32),
            pltpu.VMEM((128, 128), F32),
            pltpu.VMEM((2, 8, 128), F32),
            pltpu.VMEM((2, 8, 128), F32),
            pltpu.SemaphoreType.DMA((8,)),
            pltpu.SemaphoreType.DMA((2, 4)),
            pltpu.SemaphoreType.DMA((2,)),
            pltpu.SemaphoreType.DMA((2,)),
            pltpu.SemaphoreType.DMA((3, 2)),
            pltpu.SemaphoreType.DMA((3, 2)),
            pltpu.SemaphoreType.DMA((3, 2)),
            pltpu.SemaphoreType.DMA((3, 2)),
            pltpu.SemaphoreType.DMA((3, 4)),
            pltpu.SemaphoreType.DMA((3, 4)),
            pltpu.SemaphoreType.DMA((10,)),
            pltpu.SemaphoreType.DMA((10,)),
            pltpu.SemaphoreType.DMA((4,)),
            pltpu.SemaphoreType.DMA((4,)),
        ],
        compiler_params=pltpu.CompilerParams(
            collective_id=1, has_side_effects=True, vmem_limit_bytes=58 << 20
        ),
        name="flow_gradient",
    )(
        state_before[0], state_now[0], base_model, buoyancy, latent[0], flow_gain, flow_bias, records, source_wavelet.T,
        source_cell, shot, receiver_depth, jnp.asarray(pick, jnp.bfloat16), jnp.asarray(shift),
    )
    img, gg, bg = pl.pallas_call(
        hand_out,
        out_shape=results,
        in_specs=[any_] * 3,
        out_specs=(any_,) * 3,
        scratch_shapes=[pltpu.VMEM(r.shape, F32) for r in results] + [pltpu.SemaphoreType.DMA((2, 10))],
        name="hand_out",
    )(*made)
    return img[None], gg, bg


def solution(mesh):
    in_specs = (
        P("smp", "dom", None, None),
        P("smp", "dom", None, None),
        P("dom", None, None),
        P("dom", None, None),
        P("smp", "dom", None, None),
        P("dom", "smp", None),
        P("dom", "smp", None),
        P("dom", None, None, None),
        P(),
        P(),
        P(),
        P("dom", None),
    )
    out_specs = (P("smp", "dom", None, None), P("dom", "smp", None), P("dom", "smp", None))
    return jax.shard_map(shards, mesh=mesh, in_specs=in_specs, out_specs=out_specs, check_vma=False)
```
